256 devices in a mesh: row: 32 (over y_lo, z, core), col: 8 (over y_hi, x).
Axes of the slice: x: 4, y: 4 (y_hi: 2, y_lo: 2; y = y_hi * 2 + y_lo), z: 8, core: 2. Of those that a mesh axis runs over, the one named last changes fastest.
Arguments:
- pair: float32 [512, 512, 128], P('row', 'col'), may hold values from -6 to 6
- pair_mask: int32 [512, 512], P('row', 'col'), may hold values 0 or 1
- in_gain: float32 [128], replicated, may hold values from 0.25 to 1.75
- in_bias: float32 [128], replicated, may hold values from -3 to 3
- w_in: bfloat16 [128, 640], replicated, may hold values from -0.5 to 0.5
- out_gain: float32 [128], replicated, may hold values from 0.25 to 1.75
- out_bias: float32 [128], replicated, may hold values from -3 to 3
- w_out: bfloat16 [128, 128], replicated, may hold values from -0.5 to 0.5
- cotangent: float32 [512, 512, 128], P('row', 'col'), may hold values from -6 to 6
Outputs:
- d_pair: float32 [512, 512, 128], P('row', 'col')
- d_w_in: float32 [128, 640], replicated
- d_w_out: float32 [128, 128], replicated
The draws below stay inside these ranges and needn't reach their ends.
All inputs are finite; a program needn't handle non-finite values. No bound on the sum of `pair_mask` on one device may be relied on, other than what follows from the above.
Results may differ from the reference program's by a relative error of at most 0.014.
Values may be sent and summed in bfloat16 or wider, within the bound.
A program may use at most 128 MiB of HBM per device.

```python
import jax
import jax.numpy as jnp
from jax import lax

C = 128
H = 128
N = 512


def plant(values, key, smallest, high):
    spot = [jax.random.randint(jax.random.fold_in(key, axis), (), 0, length) for axis, length in enumerate(values.shape)]
    longest = values.shape.index(max(values.shape))
    neighbour = spot[:longest] + [(spot[longest] + 1) % values.shape[longest]] + spot[longest + 1:]
    return values.at[tuple(spot)].set(smallest).at[tuple(neighbour)].set(high)


def levels(own_key, extent, pieces, smallest, high):
    loudness = 1.0
    for position, blocks in pieces:
        heights = jax.random.uniform(jax.random.fold_in(jax.random.fold_in(own_key, 6), position), (blocks,), jnp.float32, smallest / len(pieces), high / len(pieces))
        loudness = loudness * jnp.repeat(jnp.exp(heights), extent[position] // blocks).reshape((-1,) + (1,) * (len(extent) - 1 - position))
    return loudness


def normal_values(own_key, shape, scale, bound, cuts=(), kind=jnp.bfloat16):
    values = scale * jax.random.normal(own_key, shape, jnp.float32)
    if cuts:
        values = values * levels(own_key, shape, cuts, -0.22, 0.18)
    return jnp.clip(values, -bound, bound).astype(kind)


def setup_inputs(seed: int = 0) -> dict:
    key_of = jax.random.split(jax.random.key(seed), 10)
    return {
        "pair": normal_values(key_of[0], (N, N, C), 1.0, 6.0, ((0, 32), (1, 8)), jnp.float32),
        "pair_mask": plant((jax.random.randint(key_of[1], (N, N), 0, 8) < 7).astype(jnp.int32), jax.random.fold_in(key_of[1], 1), 0, 1),
        "in_gain": jnp.clip(1.0 + 0.15 * jax.random.normal(key_of[2], (C,), jnp.float32), 0.25, 1.75),
        "in_bias": normal_values(key_of[3], (C,), 0.5, 3.0, (), jnp.float32),
        "w_in": normal_values(key_of[4], (C, 4 * H + C), C ** -0.5, 0.5),
        "out_gain": jnp.clip(1.0 + 0.15 * jax.random.normal(key_of[5], (H,), jnp.float32), 0.25, 1.75),
        "out_bias": normal_values(key_of[6], (H,), 0.5, 3.0, (), jnp.float32),
        "w_out": normal_values(key_of[7], (H, C), H ** -0.5, 0.5),
        "cotangent": normal_values(key_of[8], (N, N, C), 1.0, 6.0, ((0, 32), (1, 8)), jnp.float32),
    }


def layer_norm(values, gain, bias):
    centered = values - lax.optimization_barrier(jnp.mean(values, axis=-1, keepdims=True))
    inverse = 1.0 / jnp.sqrt(lax.optimization_barrier(jnp.mean(centered * centered, axis=-1, keepdims=True)) + 1e-05)
    normed = centered * inverse
    return (normed * gain + bias, normed, inverse)

def norm_back(normed, inverse, d_normed):
    first = lax.optimization_barrier(jnp.mean(d_normed, axis=-1, keepdims=True))
    second = lax.optimization_barrier(jnp.mean(d_normed * normed, axis=-1, keepdims=True))
    return inverse * (d_normed - first - normed * second)

def reference(pair, pair_mask, in_gain, in_bias, w_in, out_gain, out_bias, w_out, cotangent):
    width = pair.shape[2]
    hidden = w_out.shape[0]
    tokens = pair.shape[0]
    zn_full, in_normed, in_inverse = layer_norm(pair, in_gain, in_bias)
    zn_flat = zn_full.astype(jnp.bfloat16).reshape(-1, width)
    proj = jnp.dot(zn_flat, w_in, preferred_element_type=jnp.float32).reshape(tokens, tokens, -1)
    value_a = proj[:, :, 0:hidden]
    gate_a = jax.nn.sigmoid(proj[:, :, hidden:2 * hidden])
    value_b = proj[:, :, 2 * hidden:3 * hidden]
    gate_b = jax.nn.sigmoid(proj[:, :, 3 * hidden:4 * hidden])
    gate_out = jax.nn.sigmoid(proj[:, :, 4 * hidden:])
    mask_val = pair_mask.astype(jnp.float32)[:, :, None]
    left = (mask_val * gate_a * value_a).astype(jnp.bfloat16)
    right = (mask_val * gate_b * value_b).astype(jnp.bfloat16)
    left_f = left.astype(jnp.float32)
    right_f = right.astype(jnp.float32)
    product = jnp.einsum('ikh,jkh->ijh', left_f, right_f)
    xn_full, mid_normed, mid_inverse = layer_norm(product, out_gain, out_bias)
    xn_flat = xn_full.astype(jnp.bfloat16).reshape(-1, hidden)
    mixed = jnp.dot(xn_flat, w_out, preferred_element_type=jnp.float32).reshape(tokens, tokens, width)
    d_go = cotangent * mixed * gate_out * (1.0 - gate_out)
    d_mixed = (cotangent * gate_out).astype(jnp.bfloat16).reshape(-1, width)
    d_w_out = jnp.dot(xn_flat.T, d_mixed, preferred_element_type=jnp.float32)
    d_xn = jnp.dot(d_mixed, w_out.T, preferred_element_type=jnp.float32).reshape(tokens, tokens, hidden)
    d_product = norm_back(mid_normed, mid_inverse, d_xn * out_gain).astype(jnp.bfloat16)
    d_prod_f = d_product.astype(jnp.float32)
    d_left = jnp.einsum('ijh,jkh->ikh', d_prod_f, right_f)
    d_right = jnp.einsum('ijh,ikh->jkh', d_prod_f, left_f)
    d_pa = d_left * mask_val * gate_a
    d_ga = d_left * mask_val * value_a * gate_a * (1.0 - gate_a)
    d_pb = d_right * mask_val * gate_b
    d_gb = d_right * mask_val * value_b * gate_b * (1.0 - gate_b)
    d_proj = jnp.concatenate([d_pa, d_ga, d_pb, d_gb, d_go], axis=-1).astype(jnp.bfloat16).reshape(-1, 4 * hidden + width)
    d_w_in = jnp.dot(zn_flat.T, d_proj, preferred_element_type=jnp.float32)
    d_zn = jnp.dot(d_proj, w_in.T, preferred_element_type=jnp.float32).reshape(tokens, tokens, width)
    d_pair = norm_back(in_normed, in_inverse, d_zn * in_gain)
    return (d_pair, d_w_in, d_w_out)
```

```python
import functools

import jax
import jax.numpy as jnp
from jax import lax
from jax.experimental import pallas as pl
from jax.experimental.pallas import tpu as pltpu
from jax.sharding import PartitionSpec as P

BF = jnp.bfloat16
F32 = jnp.float32
COLS = 8
CHIPS = 16
T = 8
L = 128
EPS = 1e-05


def nn(a, b):
    return lax.dot_general(a, b, (((1,), (0,)), ((), ())), preferred_element_type=F32)


def nt(a, b):
    return lax.dot_general(a, b, (((1,), (1,)), ((), ())), preferred_element_type=F32)


def lanes(t):
    return pl.ds(pl.multiple_of(t * L, L), L)


def spread(vec_ref):
    return jnp.broadcast_to(vec_ref[...], (L, L)).T


def norm(x):
    cen = x - jnp.mean(x, axis=0, keepdims=True)
    inv = lax.rsqrt(jnp.mean(cen * cen, axis=0, keepdims=True) + EPS)
    return cen * inv, inv


def norm_back(normed, inv, dn):
    first = jnp.mean(dn, axis=0, keepdims=True)
    second = jnp.mean(dn * normed, axis=0, keepdims=True)
    return inv * (dn - first - normed * second)


def low_half(shape):
    return lax.broadcasted_iota(jnp.int32, shape, len(shape) - 1) < L // 2


def to_plane(src, work, out):
    for m in range(COLS // 2):
        for half in range(2):
            for t in range(T):
                work[m, half, :, t, :] = src[2 * m + half, :, t * L : (t + 1) * L].astype(F32)
    low = low_half((16, T, L))
    for m in range(COLS // 2):
        a, b = work[m, 0], work[m, 1]
        top = jnp.where(low, a, pltpu.roll(b, L // 2, 2))
        bottom = jnp.where(low, pltpu.roll(a, L // 2, 2), b)
        out[:, :, m * L : (m + 1) * L] = jnp.concatenate([top, bottom], axis=1).astype(BF)


def from_plane(src, work, out):
    low = low_half((16, T, L))
    for m in range(COLS // 2):
        x = src[:, :, m * L : (m + 1) * L].astype(F32)
        top, bottom = x[:, 0:T], x[:, T : 2 * T]
        work[m, 0] = jnp.where(low, top, pltpu.roll(bottom, L // 2, 2))
        work[m, 1] = jnp.where(low, pltpu.roll(top, L // 2, 2), bottom)
    for m in range(COLS // 2):
        for half in range(2):
            for t in range(T):
                out[2 * m + half, :, t * L : (t + 1) * L] = work[m, half, :, t, :].astype(BF)


def kernel(
    pair_ref, mask_ref, in_gain_ref, in_bias_ref, w_in_ref, out_gain_ref, out_bias_ref, w_out_ref, cot_ref,
    dpair_ref, dwin_ref, dwout_ref,
    gains, w_in_t, w_out_t, mask_rows, in_normed, in_inv, zn,
    fa1, fa2, fb1, fb2, sgo, fgo, dmix, dxn, xn, dproj,
    out_col, in_col, out_row, in_row, plane_l, plane_r, plane_d, work,
    part, part_out, part_in,
    w_send, w_recv, w_sum, w_all, w_full, w_gather,
    col_s, col_r, row_s, row_r, core_s, core_r, wt_s, wt_r,
):
    r, c = lax.axis_index("row"), lax.axis_index("col")
    q = lax.rem(r, 2)
    chip = r // 2
    mate = r + 1 - 2 * q
    flat = c * 2 + q

    barrier = pltpu.get_barrier_semaphore()

    def hello(row, col):
        pl.semaphore_signal(barrier, inc=1, device_id=(row, col), device_id_type=pl.DeviceIdType.MESH)

    @pl.loop(1, COLS)
    def _(j):
        hello(r, lax.rem(c + j, COLS))
        hello(mate, lax.rem(c + j, COLS))

    @pl.loop(1, CHIPS)
    def _(j):
        hello(2 * lax.rem(chip + j, CHIPS) + q, c)

    hello(mate, c)

    def remote(src, dst, ssem, rsem, row, col):
        return pltpu.make_async_remote_copy(
            src_ref=src, dst_ref=dst, send_sem=ssem, recv_sem=rsem,
            device_id=(row, col), device_id_type=pl.DeviceIdType.MESH,
        )

    def col_copy(n, j):
        to = lax.rem(c + j, COLS)
        return remote(out_col.at[n, to], in_col.at[n, c], col_s.at[n, j], col_r.at[n, c], r, to)

    def col_send(n):
        @pl.loop(1, COLS)
        def _(j):
            col_copy(n, j).start()

        pltpu.make_async_copy(out_col.at[n, c], in_col.at[n, c], col_r.at[n, c]).start()

    def col_wait(n):
        @pl.loop(0, COLS)
        def _(k):
            pltpu.make_async_copy(in_col.at[n, k], in_col.at[n, k], col_r.at[n, k]).wait()

    def row_copy(n, j, src, dst):
        to = lax.rem(chip + j, CHIPS)
        return remote(src(to), dst(chip), row_s.at[n, j], row_r.at[n, chip], 2 * to + q, c)

    def row_send(n, src, dst):
        @pl.loop(1, CHIPS)
        def _(j):
            row_copy(n, j, src, dst).start()

        pltpu.make_async_copy(src(chip), dst(chip), row_r.at[n, chip]).start()

    def row_wait(n, dst):
        @pl.loop(0, CHIPS)
        def _(k):
            pltpu.make_async_copy(dst(k), dst(k), row_r.at[n, k]).wait()

    def row_out(n):
        return lambda k: out_row.at[n, k]

    def row_in(n):
        return lambda k: in_row.at[n, k]

    right_rows = lambda k: plane_r.at[k, q]
    left_rows = lambda k: plane_l.at[k]
    grad_rows = lambda k: plane_d.at[k]

    gains[0] = spread(in_gain_ref)
    gains[1] = spread(in_bias_ref)
    gains[2] = spread(out_gain_ref)
    gains[3] = spread(out_bias_ref)
    w_in_t[...] = w_in_ref[...].astype(F32).T.astype(BF)
    w_out_t[...] = w_out_ref[...].astype(F32).T.astype(BF)
    mask_f = mask_ref[...].astype(F32)
    mask_rows[...] = jnp.concatenate([mask_f[0:T], mask_f[T : 2 * T]], axis=1)

    def side(t, rows, f1, f2, n):
        both = nn(w_in_t[rows : rows + 2 * L, :], zn[:, lanes(t)])
        value, gate = both[0:L], jax.nn.sigmoid(both[L : 2 * L])
        first = mask_rows[pl.ds(t, 1), :] * gate
        used = first * value
        f1[t] = first
        f2[t] = used * (1.0 - gate)
        out_col[n, :, :, lanes(t)] = used.astype(BF).reshape(COLS, 16, L)

    @pl.loop(0, T)
    def _(t):
        x = jnp.concatenate([pair_ref[t], pair_ref[t + T]], axis=0).T
        normed, inv = norm(x)
        in_normed[t] = normed
        in_inv[pl.ds(t, 1), :] = inv
        zn[:, lanes(t)] = (normed * gains[0] + gains[1]).astype(BF)
        side(t, 2 * L, fb1, fb2, 0)

    pl.semaphore_wait(barrier, 2 * (COLS - 1) + CHIPS - 1 + 1)
    col_send(0)

    @pl.loop(0, T)
    def _(t):
        side(t, 0, fa1, fa2, 1)

    col_send(1)

    col_wait(0)
    to_plane(in_col.at[0], work, out_row.at[0])
    row_send(0, row_out(0), right_rows)
    col_wait(1)
    to_plane(in_col.at[1], work, out_row.at[1])
    row_send(1, row_out(1), left_rows)

    @pl.loop(0, T)
    def _(t):
        gate = jax.nn.sigmoid(nn(w_in_t[4 * L : 5 * L, :], zn[:, lanes(t)]))
        cot = jnp.concatenate([cot_ref[t], cot_ref[t + T]], axis=0).T
        gated = cot * gate
        fgo[t] = gated * (1.0 - gate)
        mix = gated.astype(BF)
        dmix[:, lanes(t)] = mix
        dxn[t] = nn(w_out_ref[...], mix) * gains[2]

    row_wait(0, right_rows)
    swap_r = remote(plane_r.at[:, q], plane_r.at[:, q], core_s.at[0], core_r.at[0], mate, c)
    swap_r.start()
    row_wait(1, left_rows)
    pltpu.make_async_copy(plane_r.at[:, 1 - q], plane_r.at[:, 1 - q], core_r.at[0]).wait()

    out_row[2] = nt(plane_l[...].reshape(256, 512), plane_r[...].reshape(512, 512)).astype(BF).reshape(CHIPS, 16, 512)
    row_send(2, row_out(2), row_in(0))
    row_wait(2, row_in(0))
    from_plane(in_row.at[0], work, out_col.at[2])
    col_send(2)
    col_wait(2)

    @pl.loop(0, T)
    def _(t):
        normed, inv = norm(in_col[2, :, :, lanes(t)].reshape(L, L).astype(F32))
        xn[:, lanes(t)] = (normed * gains[2] + gains[3]).astype(BF)
        out_col[3, :, :, lanes(t)] = norm_back(normed, inv, dxn[t]).astype(BF).reshape(COLS, 16, L)

    col_send(3)

    @pl.loop(0, T)
    def _(t):
        dproj[4 * L : 5 * L, lanes(t)] = (fgo[t] * nn(w_out_t[...], xn[:, lanes(t)])).astype(BF)

    dwout_ref[...] = nt(xn[...], dmix[...])

    col_wait(3)
    to_plane(in_col.at[3], work, out_row.at[3])
    row_send(3, row_out(3), grad_rows)
    row_wait(3, grad_rows)

    grad = plane_d[...].reshape(256, 512)
    part[...] = nn(grad.astype(F32).T.astype(BF), plane_l[...].reshape(256, 512)).reshape(CHIPS, 2, 16, 512)
    part_out[...] = part[:, 1 - q].astype(BF)
    swap_d = remote(part_out, part_in, core_s.at[1], core_r.at[1], mate, c)
    swap_d.start()
    out_row[4] = nn(grad, plane_r[...].reshape(512, 512)).astype(BF).reshape(CHIPS, 16, 512)
    row_send(4, row_out(4), row_in(1))
    pltpu.make_async_copy(part_in, part_in, core_r.at[1]).wait()
    out_row[5] = (part[:, q] + part_in[...].astype(F32)).astype(BF)
    row_send(5, row_out(5), row_in(2))

    row_wait(4, row_in(1))
    from_plane(in_row.at[1], work, out_col.at[4])
    col_send(4)
    row_wait(5, row_in(2))
    from_plane(in_row.at[2], work, out_col.at[5])
    col_send(5)
    col_wait(4)

    @pl.loop(0, T)
    def _(t):
        d = in_col[4, :, :, lanes(t)].reshape(L, L).astype(F32)
        dproj[0:L, lanes(t)] = (d * fa1[t]).astype(BF)
        dproj[L : 2 * L, lanes(t)] = (d * fa2[t]).astype(BF)

    col_wait(5)

    @pl.loop(0, T)
    def _(t):
        d = in_col[5, :, :, lanes(t)].reshape(L, L).astype(F32)
        dproj[2 * L : 3 * L, lanes(t)] = (d * fb1[t]).astype(BF)
        dproj[3 * L : 4 * L, lanes(t)] = (d * fb2[t]).astype(BF)

    grads = jnp.concatenate([nt(zn[...], dproj[...]), dwout_ref[...]], axis=1).astype(BF)
    w_send[:, 0] = grads[:, 0 : 3 * L].reshape(COLS, 16, 3 * L)
    w_send[:, 1] = grads[:, 3 * L : 6 * L].reshape(COLS, 16, 3 * L)

    def near(j):
        to = lax.rem(flat + j, 2 * COLS)
        return to // 2, lax.rem(to, 2)

    def w1_copy(j):
        tc, tq = near(j)
        return remote(w_send.at[tc, tq], w_recv.at[flat], wt_s.at[0, j], wt_r.at[0, flat], 2 * chip + tq, tc)

    def w2_copy(j):
        to = lax.rem(chip + j, CHIPS)
        return remote(w_sum, w_all.at[chip], wt_s.at[1, j], wt_r.at[1, chip], 2 * to + q, c)

    def w3_copy(j):
        tc, tq = near(j)
        return remote(w_full, w_gather.at[c, q], wt_s.at[2, j], wt_r.at[2, flat], 2 * chip + tq, tc)

    def each(copy):
        @pl.loop(1, 16)
        def _(j):
            copy(j).start()

    each(w1_copy)
    pltpu.make_async_copy(w_send.at[c, q], w_recv.at[flat], wt_r.at[0, flat]).start()

    @pl.loop(0, T)
    def _(t):
        dn = nn(w_in_ref[...], dproj[:, lanes(t)]) * gains[0]
        d = norm_back(in_normed[t], in_inv[pl.ds(t, 1), :], dn).T
        dpair_ref[t] = d[0 : L // 2]
        dpair_ref[t + T] = d[L // 2 : L]

    @pl.loop(0, 16)
    def _(k):
        pltpu.make_async_copy(w_recv.at[k], w_recv.at[k], wt_r.at[0, k]).wait()

    w_sum[...] = jnp.sum(w_recv[...].astype(F32), axis=0).astype(BF)
    each(w2_copy)
    pltpu.make_async_copy(w_sum, w_all.at[chip], wt_r.at[1, chip]).start()

    @pl.loop(0, CHIPS)
    def _(k):
        pltpu.make_async_copy(w_all.at[k], w_all.at[k], wt_r.at[1, k]).wait()

    w_full[...] = jnp.sum(w_all[...].astype(F32), axis=0).astype(w_full.dtype)
    each(w3_copy)
    pltpu.make_async_copy(w_full, w_gather.at[c, q], wt_r.at[2, flat]).start()

    @pl.loop(0, COLS)
    def _(k):
        for core in range(2):
            pltpu.make_async_copy(w_gather.at[k, core], w_gather.at[k, core], wt_r.at[2, 2 * k + core]).wait()

    first = w_gather[:, 0].astype(F32).reshape(L, 3 * L)
    second = w_gather[:, 1].astype(F32).reshape(L, 3 * L)
    dwin_ref[:, 0 : 3 * L] = first
    dwin_ref[:, 3 * L : 5 * L] = second[:, 0 : 2 * L]
    dwout_ref[...] = second[:, 2 * L : 3 * L]

    for n in range(6):

        @pl.loop(1, COLS)
        def _(j):
            col_copy(n, j).wait_send()

    for n, dst in enumerate((right_rows, left_rows, row_in(0), grad_rows, row_in(1), row_in(2))):

        @pl.loop(1, CHIPS)
        def _(j):
            row_copy(n, j, row_out(n), dst).wait_send()

    swap_r.wait_send()
    swap_d.wait_send()

    @pl.loop(1, 16)
    def _(j):
        w1_copy(j).wait_send()
        w2_copy(j).wait_send()
        w3_copy(j).wait_send()


def body(pair, pair_mask, in_gain, in_bias, w_in, out_gain, out_bias, w_out, cotangent):
    V = pltpu.VMEM
    tile = lambda dtype: V((T, L, L), dtype)
    D = pltpu.SemaphoreType.DMA
    return pl.pallas_call(
        kernel,
        out_shape=(
            jax.ShapeDtypeStruct(pair.shape, F32),
            jax.ShapeDtypeStruct(w_in.shape, F32),
            jax.ShapeDtypeStruct(w_out.shape, F32),
        ),
        in_specs=[pl.BlockSpec(memory_space=pltpu.VMEM)] * 9,
        out_specs=[pl.BlockSpec(memory_space=pltpu.VMEM)] * 3,
        scratch_shapes=[
            V((4, L, L), F32), V((5 * L, L), BF), V((L, L), BF), V((T, L), F32), tile(F32), V((T, L), F32), V((L, T * L), BF),
            tile(F32), tile(F32), tile(F32), tile(F32), tile(F32), tile(F32), V((L, T * L), BF), tile(F32),
            V((L, T * L), BF), V((5 * L, T * L), BF),
            V((6, COLS, 16, T * L), BF), V((6, COLS, 16, T * L), BF),
            V((6, CHIPS, 16, 512), BF), V((3, CHIPS, 16, 512), BF),
            V((CHIPS, 16, 512), BF), V((CHIPS, 2, 16, 512), BF), V((CHIPS, 16, 512), BF), V((4, 2, 16, T, L), F32),
            V((CHIPS, 2, 16, 512), F32), V((CHIPS, 16, 512), BF), V((CHIPS, 16, 512), BF),
            V((COLS, 2, 16, 3 * L), BF), V((16, 16, 3 * L), BF), V((16, 3 * L), BF), V((CHIPS, 16, 3 * L), BF),
            V((16, 3 * L), F32), V((COLS, 2, 16, 3 * L), F32),
            D((6, COLS)), D((6, COLS)), D((6, CHIPS)), D((6, CHIPS)), D((2,)), D((2,)), D((3, 16)), D((3, 16)),
        ],
        compiler_params=pltpu.CompilerParams(
            collective_id=0, has_side_effects=True, vmem_limit_bytes=40 * 1024 * 1024
        ),
    )(
        pair, pair_mask, in_gain.reshape(1, L), in_bias.reshape(1, L), w_in,
        out_gain.reshape(1, L), out_bias.reshape(1, L), w_out, cotangent,
    )


def solution(mesh):
    placed = (
        P("row", "col", None),
        P("row", "col"),
        P(),
        P(),
        P(),
        P(),
        P(),
        P(),
        P("row", "col", None),
    )
    return jax.shard_map(
        body,
        mesh=mesh,
        in_specs=placed,
        out_specs=(P("row", "col", None), P(), P()),
        check_vma=False,
    )
```

```python
import functools

import jax
import jax.numpy as jnp
from jax import lax
from jax.experimental import pallas as pl
from jax.experimental.pallas import tpu as pltpu
from jax.sharding import PartitionSpec as P

BF = jnp.bfloat16
F32 = jnp.float32
COLS = 8
CHIPS = 16
DEPTH = 8
FAR_FIRST = (4, 3, 5, 2, 6, 1, 7, 0)
T = 8
L = 128
EPS = 1e-05


def nn(a, b):
    return lax.dot_general(a, b, (((1,), (0,)), ((), ())), preferred_element_type=F32)


def nt(a, b):
    return lax.dot_general(a, b, (((1,), (1,)), ((), ())), preferred_element_type=F32)


def spread(vec_ref):
    return jnp.broadcast_to(vec_ref[...], (L, L)).T


def norm(x):
    cen = x - jnp.mean(x, axis=0, keepdims=True)
    inv = lax.rsqrt(jnp.mean(cen * cen, axis=0, keepdims=True) + EPS)
    return cen * inv, inv


def norm_back(normed, inv, dn):
    first = jnp.mean(dn, axis=0, keepdims=True)
    second = jnp.mean(dn * normed, axis=0, keepdims=True)
    return inv * (dn - first - normed * second)


def low_half(shape):
    return lax.broadcasted_iota(jnp.int32, shape, len(shape) - 1) < L // 2


def join(src, m):
    low = low_half((CHIPS, T, L))
    a, b = src[:, 2 * m].astype(F32), src[:, 2 * m + 1].astype(F32)
    top = jnp.where(low, a, pltpu.roll(b, L // 2, 2))
    bottom = jnp.where(low, pltpu.roll(a, L // 2, 2), b)
    return jnp.concatenate([top, bottom], axis=1).astype(BF)


def split(x, out, m):
    low = low_half((CHIPS, T, L))
    x = x.reshape(CHIPS, 2 * T, L)
    top, bottom = x[:, 0:T], x[:, T : 2 * T]
    out[:, 2 * m] = jnp.where(low, top, pltpu.roll(bottom, L // 2, 2)).astype(BF)
    out[:, 2 * m + 1] = jnp.where(low, pltpu.roll(top, L // 2, 2), bottom).astype(BF)


def kernel(
    pair_ref, mask_ref, in_gain_ref, in_bias_ref, w_in_ref, out_gain_ref, out_bias_ref, w_out_ref, cot_ref,
    dpair_ref, dwin_ref, dwout_ref,
    gains, w_in_t, w_out_t, mask_rows, in_normed, in_inv, zn,
    fa1, fa2, fb1, fb2, fgo, dmix, dxn, xn, dproj, dwout,
    out_h, in_h, out_p, in_p, plane_l, plane_r, plane_d, grad_t, work_r, work_l,
    part_out, part_in,
    w_send, w_recv, w_sum, w_all, w_full, w_gather,
    leg_s, leg_r, core_s, core_r, wt_s, wt_r,
):
    r, c = lax.axis_index("row"), lax.axis_index("col")
    q = lax.rem(r, 2)
    chip = r // 2
    y, z = chip // DEPTH, lax.rem(chip, DEPTH)
    mate = r + 1 - 2 * q
    me = chip * COLS + c
    flat = (c * 2 + y) * 2 + q

    def every_chip(act):
        for dz in FAR_FIRST:

            @pl.loop(0 if dz else 1, 16)
            def _(k):
                to_y = lax.rem(y + k // COLS, 2)
                to_c = lax.rem(c + lax.rem(k, COLS), COLS)
                act(to_y * DEPTH + lax.rem(z + dz, DEPTH), to_c)

    barrier = pltpu.get_barrier_semaphore()

    def hello(row, col):
        pl.semaphore_signal(barrier, inc=1, device_id=(row, col), device_id_type=pl.DeviceIdType.MESH)

    every_chip(lambda to, col: hello(2 * to + q, col))

    @pl.loop(0, 16)
    def _(k):
        to_y = lax.rem(y + k // COLS, 2)
        hello(2 * (to_y * DEPTH + z) + 1 - q, lax.rem(c + lax.rem(k, COLS), COLS))

    def remote(src, dst, ssem, rsem, row, col):
        return pltpu.make_async_remote_copy(
            src_ref=src, dst_ref=dst, send_sem=ssem, recv_sem=rsem,
            device_id=(row, col), device_id_type=pl.DeviceIdType.MESH,
        )

    sent = []

    def leg_send(n, src, dst):
        every_chip(
            lambda to, col: remote(
                src.at[to * COLS + col], dst.at[me], leg_s.at[n], leg_r.at[n], 2 * to + q, col
            ).start()
        )
        pltpu.make_async_copy(src.at[me], dst.at[me], leg_r.at[n]).start()
        rest = src.at[0 : CHIPS * COLS - 1]
        sent.append(pltpu.make_async_copy(rest, rest, leg_s.at[n]).wait)

    def leg_wait(n, dst):
        pltpu.make_async_copy(dst, dst, leg_r.at[n]).wait()

    def blocks(ref):
        return ref[...].reshape(CHIPS, COLS, T, L)

    gains[0] = spread(in_gain_ref)
    gains[1] = spread(in_bias_ref)
    gains[2] = spread(out_gain_ref)
    gains[3] = spread(out_bias_ref)
    w_in_t[...] = w_in_ref[...].astype(F32).T.astype(BF)
    w_out_t[...] = w_out_ref[...].astype(F32).T.astype(BF)
    mask_f = mask_ref[...].astype(F32)
    mask_rows[...] = jnp.concatenate([mask_f[0:T], mask_f[T : 2 * T]], axis=1)

    def side(t, rows, f1, f2, work):
        both = nn(w_in_t[rows : rows + 2 * L, :], zn[:, t * L : (t + 1) * L])
        value, gate = both[0:L], jax.nn.sigmoid(both[L : 2 * L])
        first = mask_rows[t : t + 1, :] * gate
        used = first * value
        f1[t] = first
        f2[t] = used * (1.0 - gate)
        work[:, t, :] = used

    for t in range(T):
        x = jnp.concatenate([pair_ref[t], pair_ref[t + T]], axis=0).T
        normed, inv = norm(x)
        in_normed[t] = normed
        in_inv[t : t + 1, :] = inv
        zn[:, t * L : (t + 1) * L] = (normed * gains[0] + gains[1]).astype(BF)
        side(t, 2 * L, fb1, fb2, work_r)
    out_h[0] = work_r[...].astype(BF)

    pl.semaphore_wait(barrier, CHIPS * COLS - 1 + 16)
    leg_send(0, out_h.at[0], in_p.at[0])

    for t in range(T):
        side(t, 0, fa1, fa2, work_l)
    out_h[1] = work_l[...].astype(BF)
    leg_send(1, out_h.at[1], in_p.at[1])

    for t in range(T):
        gate = jax.nn.sigmoid(nn(w_in_t[4 * L : 5 * L, :], zn[:, t * L : (t + 1) * L]))
        cot = jnp.concatenate([cot_ref[t], cot_ref[t + T]], axis=0).T
        gated = cot * gate
        fgo[t] = gated * (1.0 - gate)
        mix = gated.astype(BF)
        dmix[:, t * L : (t + 1) * L] = mix
        dxn[:, t, :] = nn(w_out_ref[...], mix) * gains[2]

    leg_wait(0, in_p.at[0])
    for m in range(COLS // 2):
        plane_r[:, q, :, m * L : (m + 1) * L] = join(blocks(in_p.at[0]), m)
    swap_r = remote(plane_r.at[:, q], plane_r.at[:, q], core_s.at[0], core_r.at[0], mate, c)
    swap_r.start()
    sent.append(swap_r.wait_send)
    leg_wait(1, in_p.at[1])
    for m in range(COLS // 2):
        plane_l[:, :, m * L : (m + 1) * L] = join(blocks(in_p.at[1]), m)
    pltpu.make_async_copy(plane_r.at[:, 1 - q], plane_r.at[:, 1 - q], core_r.at[0]).wait()

    for m in range(COLS // 2):
        rows = plane_r[4 * m : 4 * m + 4].reshape(L, 512)
        split(nt(plane_l[...].reshape(256, 512), rows), out_p.at[0], m)
    leg_send(2, out_p.at[0].reshape(CHIPS * COLS, T, L), in_h.at[0])
    leg_wait(2, in_h.at[0])

    normed, inv = norm(in_h[0].astype(F32))
    work_r[...] = normed
    out_h[2] = norm_back(normed, inv, dxn[...]).astype(BF)
    leg_send(3, out_h.at[2], in_p.at[2])

    for t in range(T):
        some = (work_r[:, t, :] * gains[2] + gains[3]).astype(BF)
        xn[:, t * L : (t + 1) * L] = some
        dproj[4 * L : 5 * L, t * L : (t + 1) * L] = (fgo[t] * nn(w_out_t[...], some)).astype(BF)
    dwout[...] = nt(xn[...], dmix[...])

    leg_wait(3, in_p.at[2])
    for m in range(COLS // 2):
        some = join(blocks(in_p.at[2]), m)
        plane_d[:, :, m * L : (m + 1) * L] = some
        grad_t[4 * m : 4 * m + 4] = some.reshape(256, L).astype(F32).T.astype(BF).reshape(4, 2, 16, 256)

    part_out[...] = nn(grad_t[:, 1 - q].reshape(256, 256), plane_l[...].reshape(256, 512)).astype(BF)
    swap_d = remote(part_out, part_in, core_s.at[1], core_r.at[1], mate, c)
    swap_d.start()
    sent.append(swap_d.wait_send)
    for m in range(COLS // 2):
        cols = plane_r[:, :, :, m * L : (m + 1) * L].reshape(512, L)
        split(nn(plane_d[...].reshape(256, 512), cols), out_p.at[1], m)
    leg_send(4, out_p.at[1].reshape(CHIPS * COLS, T, L), in_h.at[1])
    pltpu.make_async_copy(part_in, part_in, core_r.at[1]).wait()
    for m in range(COLS // 2):
        cols = plane_l[:, :, m * L : (m + 1) * L].reshape(256, L)
        own = nn(grad_t[:, q].reshape(256, 256), cols)
        split(own + part_in[:, m * L : (m + 1) * L].astype(F32), out_p.at[2], m)
    leg_send(5, out_p.at[2].reshape(CHIPS * COLS, T, L), in_h.at[2])

    leg_wait(4, in_h.at[1])
    work_l[...] = in_h[1].astype(F32)
    for t in range(T):
        d = work_l[:, t, :]
        dproj[0:L, t * L : (t + 1) * L] = (d * fa1[t]).astype(BF)
        dproj[L : 2 * L, t * L : (t + 1) * L] = (d * fa2[t]).astype(BF)
    leg_wait(5, in_h.at[2])
    work_r[...] = in_h[2].astype(F32)
    for t in range(T):
        d = work_r[:, t, :]
        dproj[2 * L : 3 * L, t * L : (t + 1) * L] = (d * fb1[t]).astype(BF)
        dproj[3 * L : 4 * L, t * L : (t + 1) * L] = (d * fb2[t]).astype(BF)

    grads = jnp.concatenate([nt(zn[...], dproj[...]), dwout[...]], axis=1).astype(BF)
    w_send[:, 0] = grads[:, 0 : 3 * L].reshape(16, 8, 3 * L)
    w_send[:, 1] = grads[:, 3 * L : 6 * L].reshape(16, 8, 3 * L)

    def near(j):
        to = lax.rem(flat + j, 32)
        return to // 2, lax.rem(to, 2), 2 * (lax.rem(to // 2, 2) * DEPTH + z) + lax.rem(to, 2), to // 4

    def w1_copy(j):
        block, core, row, col = near(j)
        return remote(w_send.at[block, core], w_recv.at[flat], wt_s.at[0], wt_r.at[0], row, col)

    def w2_copy(j):
        row = 2 * (y * DEPTH + lax.rem(z + j, DEPTH)) + q
        return remote(w_sum, w_all.at[z], wt_s.at[1], wt_r.at[1], row, c)

    def w3_copy(j):
        block, core, row, col = near(j)
        return remote(w_full, w_gather.at[flat], wt_s.at[2], wt_r.at[2], row, col)

    def each(copy, count, n, whole):
        @pl.loop(1, count)
        def _(j):
            copy(j).start()

        rest = whole.at[0 : count - 1]
        sent.append(pltpu.make_async_copy(rest, rest, wt_s.at[n]).wait)

    each(w1_copy, 32, 0, w_recv)
    pltpu.make_async_copy(w_send.at[c * 2 + y, q], w_recv.at[flat], wt_r.at[0]).start()

    for t in range(T):
        dn = nn(w_in_ref[...], dproj[:, t * L : (t + 1) * L]) * gains[0]
        d = norm_back(in_normed[t], in_inv[t : t + 1, :], dn).T
        dpair_ref[t] = d[0 : L // 2]
        dpair_ref[t + T] = d[L // 2 : L]

    pltpu.make_async_copy(w_recv, w_recv, wt_r.at[0]).wait()
    w_sum[...] = jnp.sum(w_recv[...].astype(F32), axis=0).astype(BF)
    each(w2_copy, DEPTH, 1, w_all)
    pltpu.make_async_copy(w_sum, w_all.at[z], wt_r.at[1]).start()
    pltpu.make_async_copy(w_all, w_all, wt_r.at[1]).wait()
    w_full[...] = jnp.sum(w_all[...].astype(F32), axis=0).astype(BF)
    each(w3_copy, 32, 2, w_gather)
    pltpu.make_async_copy(w_full, w_gather.at[flat], wt_r.at[2]).start()
    pltpu.make_async_copy(w_gather, w_gather, wt_r.at[2]).wait()

    whole = w_gather[...].astype(F32).reshape(16, 2, 8, 3 * L)
    first, second = whole[:, 0].reshape(L, 3 * L), whole[:, 1].reshape(L, 3 * L)
    dwin_ref[:, 0 : 3 * L] = first
    dwin_ref[:, 3 * L : 5 * L] = second[:, 0 : 2 * L]
    dwout_ref[...] = second[:, 2 * L : 3 * L]

    for wait in sent:
        wait()


def body(pair, pair_mask, in_gain, in_bias, w_in, out_gain, out_bias, w_out, cotangent):
    V = pltpu.VMEM
    tile = lambda dtype: V((T, L, L), dtype)
    D = pltpu.SemaphoreType.DMA
    return pl.pallas_call(
        kernel,
        out_shape=(
            jax.ShapeDtypeStruct(pair.shape, F32),
            jax.ShapeDtypeStruct(w_in.shape, F32),
            jax.ShapeDtypeStruct(w_out.shape, F32),
        ),
        in_specs=[pl.BlockSpec(memory_space=pltpu.VMEM)] * 9,
        out_specs=[pl.BlockSpec(memory_space=pltpu.VMEM)] * 3,
        scratch_shapes=[
            V((4, L, L), F32), V((5 * L, L), BF), V((L, L), BF), V((T, L), F32), tile(F32), V((T, L), F32), V((L, T * L), BF),
            tile(F32), tile(F32), tile(F32), tile(F32), tile(F32), V((L, T * L), BF), V((L, T, L), F32),
            V((L, T * L), BF), V((5 * L, T * L), BF), V((L, L), F32),
            V((3, L, T, L), BF), V((3, L, T, L), BF),
            V((3, CHIPS, COLS, T, L), BF), V((3, L, T, L), BF),
            V((CHIPS, 16, 512), BF), V((CHIPS, 2, 16, 512), BF), V((CHIPS, 16, 512), BF), V((CHIPS, 2, 16, 256), BF),
            V((L, T, L), F32), V((L, T, L), F32),
            V((256, 512), BF), V((256, 512), BF),
            V((16, 2, 8, 3 * L), BF), V((32, 8, 3 * L), BF), V((8, 3 * L), BF), V((DEPTH, 8, 3 * L), BF),
            V((8, 3 * L), BF), V((32, 8, 3 * L), BF),
            D((6,)), D((6,)), D((2,)), D((2,)), D((3,)), D((3,)),
        ],
        compiler_params=pltpu.CompilerParams(
            collective_id=0, has_side_effects=True, vmem_limit_bytes=60 * 1024 * 1024
        ),
    )(
        pair, pair_mask, in_gain.reshape(1, L), in_bias.reshape(1, L), w_in,
        out_gain.reshape(1, L), out_bias.reshape(1, L), w_out, cotangent,
    )


def solution(mesh):
    placed = (
        P("row", "col", None),
        P("row", "col"),
        P(),
        P(),
        P(),
        P(),
        P(),
        P(),
        P("row", "col", None),
    )
    return jax.shard_map(
        body,
        mesh=mesh,
        in_specs=placed,
        out_specs=(P("row", "col", None), P(), P()),
        check_vma=False,
    )
```

```python
import functools

import jax
import jax.numpy as jnp
from jax import lax
from jax.experimental import pallas as pl
from jax.experimental.pallas import tpu as pltpu
from jax.sharding import PartitionSpec as P

BF = jnp.bfloat16
F32 = jnp.float32
COLS = 8
CHIPS = 16
DEPTH = 8
FAR_FIRST = (4, 3, 5, 2, 6, 1, 7, 0)
UNROLL = 3
T = 8
L = 128
EPS = 1e-05


def nn(a, b):
    return lax.dot_general(a, b, (((1,), (0,)), ((), ())), preferred_element_type=F32)


def nt(a, b):
    return lax.dot_general(a, b, (((1,), (1,)), ((), ())), preferred_element_type=F32)


def spread(vec_ref):
    return jnp.broadcast_to(vec_ref[...], (L, L)).T


def norm(x):
    cen = x - jnp.mean(x, axis=0, keepdims=True)
    inv = lax.rsqrt(jnp.mean(cen * cen, axis=0, keepdims=True) + EPS)
    return cen * inv, inv


def norm_back(normed, inv, dn):
    first = jnp.mean(dn, axis=0, keepdims=True)
    second = jnp.mean(dn * normed, axis=0, keepdims=True)
    return inv * (dn - first - normed * second)


def low_half(shape):
    return lax.broadcasted_iota(jnp.int32, shape, len(shape) - 1) < L // 2


def join(src, m):
    low = low_half((CHIPS, T, L))
    a, b = src[:, 2 * m].astype(F32), src[:, 2 * m + 1].astype(F32)
    top = jnp.where(low, a, pltpu.roll(b, L // 2, 2))
    bottom = jnp.where(low, pltpu.roll(a, L // 2, 2), b)
    return jnp.concatenate([top, bottom], axis=1).astype(BF)


def split(x, out, m):
    low = low_half((CHIPS, T, L))
    x = x.reshape(CHIPS, 2 * T, L)
    top, bottom = x[:, 0:T], x[:, T : 2 * T]
    out[:, 2 * m] = jnp.where(low, top, pltpu.roll(bottom, L // 2, 2)).astype(BF)
    out[:, 2 * m + 1] = jnp.where(low, pltpu.roll(top, L // 2, 2), bottom).astype(BF)


def kernel(
    pair_hbm, mask_ref, in_gain_ref, in_bias_ref, w_in_hbm, out_gain_ref, out_bias_ref, w_out_hbm, cot_hbm,
    dpair_hbm, gather_ref,
    pair_ref, w_in_ref, w_out_ref, cot_ref, dpair_ref, io_sem,
    gains, w_in_t, w_out_t, mask_rows, in_normed, in_inv, zn,
    fa1, fa2, fb1, fb2, fgo, dmix, dxn, xn, dproj, dwout,
    out_h2, in_p2, out_p, in_h, out_h, in_p, out_p2, in_h2, plane_l, plane_r, plane_d, grad_t, work_r, work_l,
    part_out, part_in,
    w_send, w_recv, w_sum, w_all, w_full, w_gather,
    leg_s, leg_r, core_s, core_r, wt_s, wt_r,
):
    r, c = lax.axis_index("row"), lax.axis_index("col")
    q = lax.rem(r, 2)
    chip = r // 2
    y, z = chip // DEPTH, lax.rem(chip, DEPTH)
    mate = r + 1 - 2 * q
    me = chip * COLS + c
    flat = (c * 2 + y) * 2 + q

    loads = [
        pltpu.make_async_copy(src, dst, io_sem.at[n])
        for n, (src, dst) in enumerate(
            ((pair_hbm, pair_ref), (w_in_hbm, w_in_ref), (w_out_hbm, w_out_ref), (cot_hbm, cot_ref))
        )
    ]
    for load in loads:
        load.start()

    levels = [lax.rem(z + dz, DEPTH) for dz in FAR_FIRST]

    def every_chip(act):
        for level in levels[:-1]:
            act(y * DEPTH + level, c)

        @pl.loop(1, 16, unroll=UNROLL)
        def _(k):
            k = 16 - k
            base = lax.rem(y + k // COLS, 2) * DEPTH
            col = lax.rem(c + lax.rem(k, COLS), COLS)
            for level in levels:
                act(base + level, col)

    barrier = pltpu.get_barrier_semaphore()

    def hello(row, col):
        pl.semaphore_signal(barrier, inc=1, device_id=(row, col), device_id_type=pl.DeviceIdType.MESH)

    every_chip(lambda to, col: hello(2 * to + q, col))

    @pl.loop(0, 16)
    def _(k):
        to_y = lax.rem(y + k // COLS, 2)
        hello(2 * (to_y * DEPTH + z) + 1 - q, lax.rem(c + lax.rem(k, COLS), COLS))

    def remote(src, dst, ssem, rsem, row, col):
        return pltpu.make_async_remote_copy(
            src_ref=src, dst_ref=dst, send_sem=ssem, recv_sem=rsem,
            device_id=(row, col), device_id_type=pl.DeviceIdType.MESH,
        )

    sent = []

    def leg_send(n, src, dst):
        every_chip(
            lambda to, col: remote(
                src.at[to * COLS + col], dst.at[me], leg_s.at[n], leg_r.at[n], 2 * to + q, col
            ).start()
        )
        pltpu.make_async_copy(src.at[me], dst.at[me], leg_r.at[n]).start()
        rest = src.at[0 : CHIPS * COLS - 1]
        sent.append(pltpu.make_async_copy(rest, rest, leg_s.at[n]).wait)

    def leg_wait(n, dst):
        pltpu.make_async_copy(dst, dst, leg_r.at[n]).wait()

    def pair_blocks(side):
        return in_p2[:, side].reshape(CHIPS, COLS, T, L)

    gains[0] = spread(in_gain_ref)
    gains[1] = spread(in_bias_ref)
    gains[2] = spread(out_gain_ref)
    gains[3] = spread(out_bias_ref)
    for load in loads[:3]:
        load.wait()
    w_in_t[...] = w_in_ref[...].astype(F32).T.astype(BF)
    w_out_t[...] = w_out_ref[...].astype(F32).T.astype(BF)
    mask_f = mask_ref[...].astype(F32)
    mask_rows[...] = jnp.concatenate([mask_f[0:T], mask_f[T : 2 * T]], axis=1)

    def side(t, rows, f1, f2, work):
        both = nn(w_in_t[rows : rows + 2 * L, :], zn[:, t * L : (t + 1) * L])
        value, gate = both[0:L], jax.nn.sigmoid(both[L : 2 * L])
        first = mask_rows[t : t + 1, :] * gate
        used = first * value
        f1[t] = first
        f2[t] = used * (1.0 - gate)
        work[:, t, :] = used

    for t in range(T):
        x = jnp.concatenate([pair_ref[t], pair_ref[t + T]], axis=0).T
        normed, inv = norm(x)
        in_normed[t] = normed
        in_inv[t : t + 1, :] = inv
        zn[:, t * L : (t + 1) * L] = (normed * gains[0] + gains[1]).astype(BF)
        side(t, 2 * L, fb1, fb2, work_r)
    out_h2[:, 0] = work_r[...].astype(BF)

    for t in range(T):
        side(t, 0, fa1, fa2, work_l)
    out_h2[:, 1] = work_l[...].astype(BF)

    pl.semaphore_wait(barrier, CHIPS * COLS - 1 + 16)
    leg_send(0, out_h2, in_p2)

    loads[3].wait()
    for t in range(T):
        gate = jax.nn.sigmoid(nn(w_in_t[4 * L : 5 * L, :], zn[:, t * L : (t + 1) * L]))
        cot = jnp.concatenate([cot_ref[t], cot_ref[t + T]], axis=0).T
        gated = cot * gate
        fgo[t] = gated * (1.0 - gate)
        mix = gated.astype(BF)
        dmix[:, t * L : (t + 1) * L] = mix
        dxn[:, t, :] = nn(w_out_ref[...], mix) * gains[2]

    leg_wait(0, in_p2)
    for m in range(COLS // 2):
        plane_r[:, q, :, m * L : (m + 1) * L] = join(pair_blocks(0), m)
    swap_r = remote(plane_r.at[:, q], plane_r.at[:, q], core_s.at[0], core_r.at[0], mate, c)
    swap_r.start()
    sent.append(swap_r.wait_send)
    for m in range(COLS // 2):
        plane_l[:, :, m * L : (m + 1) * L] = join(pair_blocks(1), m)
    pltpu.make_async_copy(plane_r.at[:, 1 - q], plane_r.at[:, 1 - q], core_r.at[0]).wait()

    for m in range(COLS // 2):
        rows = plane_r[4 * m : 4 * m + 4].reshape(L, 512)
        split(nt(plane_l[...].reshape(256, 512), rows), out_p, m)
    leg_send(1, out_p.reshape(CHIPS * COLS, T, L), in_h)
    leg_wait(1, in_h)

    normed, inv = norm(in_h[...].astype(F32))
    work_r[...] = normed
    out_h[...] = norm_back(normed, inv, dxn[...]).astype(BF)
    leg_send(2, out_h, in_p)

    for t in range(T):
        some = (work_r[:, t, :] * gains[2] + gains[3]).astype(BF)
        xn[:, t * L : (t + 1) * L] = some
        dproj[4 * L : 5 * L, t * L : (t + 1) * L] = (fgo[t] * nn(w_out_t[...], some)).astype(BF)
    dwout[...] = nt(xn[...], dmix[...])

    leg_wait(2, in_p)
    for m in range(COLS // 2):
        some = join(in_p[...].reshape(CHIPS, COLS, T, L), m)
        plane_d[:, :, m * L : (m + 1) * L] = some
        grad_t[4 * m : 4 * m + 4] = some.reshape(256, L).astype(F32).T.astype(BF).reshape(4, 2, 16, 256)

    part_out[...] = nn(grad_t[:, 1 - q].reshape(256, 256), plane_l[...].reshape(256, 512)).astype(BF)
    swap_d = remote(part_out, part_in, core_s.at[1], core_r.at[1], mate, c)
    swap_d.start()
    sent.append(swap_d.wait_send)
    for m in range(COLS // 2):
        cols = plane_r[:, :, :, m * L : (m + 1) * L].reshape(512, L)
        split(nn(plane_d[...].reshape(256, 512), cols), out_p2.at[:, :, 0], m)
    pltpu.make_async_copy(part_in, part_in, core_r.at[1]).wait()
    for m in range(COLS // 2):
        cols = plane_l[:, :, m * L : (m + 1) * L].reshape(256, L)
        own = nn(grad_t[:, q].reshape(256, 256), cols)
        split(own + part_in[:, m * L : (m + 1) * L].astype(F32), out_p2.at[:, :, 1], m)
    leg_send(3, out_p2.reshape(CHIPS * COLS, 2, T, L), in_h2)

    leg_wait(3, in_h2)
    work_l[...] = in_h2[:, 0].astype(F32)
    work_r[...] = in_h2[:, 1].astype(F32)
    for t in range(T):
        d = work_l[:, t, :]
        dproj[0:L, t * L : (t + 1) * L] = (d * fa1[t]).astype(BF)
        dproj[L : 2 * L, t * L : (t + 1) * L] = (d * fa2[t]).astype(BF)
    for t in range(T):
        d = work_r[:, t, :]
        dproj[2 * L : 3 * L, t * L : (t + 1) * L] = (d * fb1[t]).astype(BF)
        dproj[3 * L : 4 * L, t * L : (t + 1) * L] = (d * fb2[t]).astype(BF)

    grads = jnp.concatenate([nt(zn[...], dproj[...]), dwout[...]], axis=1).astype(BF)
    w_send[:, 0] = grads[:, 0 : 3 * L].reshape(16, 8, 3 * L)
    w_send[:, 1] = grads[:, 3 * L : 6 * L].reshape(16, 8, 3 * L)

    def near(j):
        to = lax.rem(flat + j, 32)
        return to // 2, lax.rem(to, 2), 2 * (lax.rem(to // 2, 2) * DEPTH + z) + lax.rem(to, 2), to // 4

    def w1_copy(j):
        block, core, row, col = near(j)
        return remote(w_send.at[block, core], w_recv.at[flat], wt_s.at[0], wt_r.at[0], row, col)

    def w2_copy(j):
        row = 2 * (y * DEPTH + lax.rem(z + j, DEPTH)) + q
        return remote(w_sum, w_all.at[z], wt_s.at[1], wt_r.at[1], row, c)

    def w3_copy(j):
        block, core, row, col = near(j)
        return remote(w_full, w_gather.at[flat], wt_s.at[2], wt_r.at[2], row, col)

    def each(copy, count, n, whole):
        @pl.loop(1, count)
        def _(j):
            copy(j).start()

        rest = whole.at[0 : count - 1]
        sent.append(pltpu.make_async_copy(rest, rest, wt_s.at[n]).wait)

    each(w1_copy, 32, 0, w_recv)
    pltpu.make_async_copy(w_send.at[c * 2 + y, q], w_recv.at[flat], wt_r.at[0]).start()

    for t in range(T):
        dn = nn(w_in_ref[...], dproj[:, t * L : (t + 1) * L]) * gains[0]
        d = norm_back(in_normed[t], in_inv[t : t + 1, :], dn).T
        dpair_ref[t] = d[0 : L // 2]
        dpair_ref[t + T] = d[L // 2 : L]

    store = pltpu.make_async_copy(dpair_ref, dpair_hbm, io_sem.at[4])
    store.start()
    pltpu.make_async_copy(w_recv, w_recv, wt_r.at[0]).wait()
    w_sum[...] = jnp.sum(w_recv[...].astype(F32), axis=0).astype(BF)
    each(w2_copy, DEPTH, 1, w_all)
    pltpu.make_async_copy(w_sum, w_all.at[z], wt_r.at[1]).start()
    pltpu.make_async_copy(w_all, w_all, wt_r.at[1]).wait()
    w_full[...] = jnp.sum(w_all[...].astype(F32), axis=0).astype(BF)
    each(w3_copy, 32, 2, w_gather)
    pltpu.make_async_copy(w_full, w_gather.at[flat], wt_r.at[2]).start()
    pltpu.make_async_copy(w_gather, w_gather, wt_r.at[2]).wait()

    gather_ref[...] = w_gather[...]
    store.wait()

    for wait in sent:
        wait()


def finish_kernel(dpair_in, gather_ref, dpair_out, dwin_ref, dwout_ref, sem):
    move = pltpu.make_async_copy(dpair_in, dpair_out, sem)
    move.start()
    whole = gather_ref[...].astype(F32).reshape(16, 2, 8, 3 * L)
    first, second = whole[:, 0].reshape(L, 3 * L), whole[:, 1].reshape(L, 3 * L)
    dwin_ref[:, 0 : 3 * L] = first
    dwin_ref[:, 3 * L : 5 * L] = second[:, 0 : 2 * L]
    dwout_ref[...] = second[:, 2 * L : 3 * L]
    move.wait()


def body(pair, pair_mask, in_gain, in_bias, w_in, out_gain, out_bias, w_out, cotangent):
    V = pltpu.VMEM
    tile = lambda dtype: V((T, L, L), dtype)
    D = pltpu.SemaphoreType.DMA
    vmem, hbm = pl.BlockSpec(memory_space=pltpu.VMEM), pl.BlockSpec(memory_space=pl.ANY)
    d_pair, gathered = pl.pallas_call(
        kernel,
        out_shape=(jax.ShapeDtypeStruct(pair.shape, F32), jax.ShapeDtypeStruct((32, 8, 3 * L), BF)),
        in_specs=[hbm, vmem, vmem, vmem, hbm, vmem, vmem, hbm, hbm],
        out_specs=(hbm, vmem),
        scratch_shapes=[
            V(pair.shape, F32), V(w_in.shape, BF), V(w_out.shape, BF), V(pair.shape, F32), V(pair.shape, F32), D((5,)),
            V((4, L, L), F32), V((5 * L, L), BF), V((L, L), BF), V((T, L), F32), tile(F32), V((T, L), F32), V((L, T * L), BF),
            tile(F32), tile(F32), tile(F32), tile(F32), tile(F32), V((L, T * L), BF), V((L, T, L), F32),
            V((L, T * L), BF), V((5 * L, T * L), BF), V((L, L), F32),
            V((L, 2, T, L), BF), V((L, 2, T, L), BF), V((CHIPS, COLS, T, L), BF), V((L, T, L), BF),
            V((L, T, L), BF), V((L, T, L), BF), V((CHIPS, COLS, 2, T, L), BF), V((L, 2, T, L), BF),
            V((CHIPS, 16, 512), BF), V((CHIPS, 2, 16, 512), BF), V((CHIPS, 16, 512), BF), V((CHIPS, 2, 16, 256), BF),
            V((L, T, L), F32), V((L, T, L), F32),
            V((256, 512), BF), V((256, 512), BF),
            V((16, 2, 8, 3 * L), BF), V((32, 8, 3 * L), BF), V((8, 3 * L), BF), V((DEPTH, 8, 3 * L), BF),
            V((8, 3 * L), BF), V((32, 8, 3 * L), BF),
            D((4,)), D((4,)), D((2,)), D((2,)), D((3,)), D((3,)),
        ],
        compiler_params=pltpu.CompilerParams(
            collective_id=0, has_side_effects=True, vmem_limit_bytes=60 * 1024 * 1024
        ),
    )(
        pair, pair_mask, in_gain.reshape(1, L), in_bias.reshape(1, L), w_in,
        out_gain.reshape(1, L), out_bias.reshape(1, L), w_out, cotangent,
    )
    return pl.pallas_call(
        finish_kernel,
        out_shape=(
            jax.ShapeDtypeStruct(pair.shape, F32),
            jax.ShapeDtypeStruct(w_in.shape, F32),
            jax.ShapeDtypeStruct(w_out.shape, F32),
        ),
        in_specs=[hbm, vmem],
        out_specs=(hbm, vmem, vmem),
        scratch_shapes=[D],
    )(d_pair, gathered)


def solution(mesh):
    placed = (
        P("row", "col", None),
        P("row", "col"),
        P(),
        P(),
        P(),
        P(),
        P(),
        P(),
        P("row", "col", None),
    )
    return jax.shard_map(
        body,
        mesh=mesh,
        in_specs=placed,
        out_specs=(P("row", "col", None), P(), P()),
        check_vma=False,
    )
```

```python
import functools

import jax
import jax.numpy as jnp
from jax import lax
from jax.experimental import pallas as pl
from jax.experimental.pallas import tpu as pltpu
from jax.sharding import PartitionSpec as P

BF = jnp.bfloat16
F32 = jnp.float32
COLS = 8
CHIPS = 16
DEPTH = 8
FAR_FIRST = (4, 3, 5, 2, 6, 1, 7, 0)
UNROLL = 3
T = 8
L = 128
EPS = 1e-05


def nn(a, b):
    return lax.dot_general(a, b, (((1,), (0,)), ((), ())), preferred_element_type=F32)


def nt(a, b):
    return lax.dot_general(a, b, (((1,), (1,)), ((), ())), preferred_element_type=F32)


def spread(vec_ref):
    return jnp.broadcast_to(vec_ref[...], (L, L)).T


def norm(x):
    cen = x - jnp.mean(x, axis=0, keepdims=True)
    inv = lax.rsqrt(jnp.mean(cen * cen, axis=0, keepdims=True) + EPS)
    return cen * inv, inv


def norm_back(normed, inv, dn):
    first = jnp.mean(dn, axis=0, keepdims=True)
    second = jnp.mean(dn * normed, axis=0, keepdims=True)
    return inv * (dn - first - normed * second)


def low_half(shape):
    return lax.broadcasted_iota(jnp.int32, shape, len(shape) - 1) < L // 2


def join(src, m):
    low = low_half((CHIPS, T, L))
    a, b = src[:, 2 * m].astype(F32), src[:, 2 * m + 1].astype(F32)
    top = jnp.where(low, a, pltpu.roll(b, L // 2, 2))
    bottom = jnp.where(low, pltpu.roll(a, L // 2, 2), b)
    return jnp.concatenate([top, bottom], axis=1).astype(BF)


def split(x, out, m):
    low = low_half((CHIPS, T, L))
    x = x.reshape(CHIPS, 2 * T, L)
    top, bottom = x[:, 0:T], x[:, T : 2 * T]
    out[:, 2 * m] = jnp.where(low, top, pltpu.roll(bottom, L // 2, 2)).astype(BF)
    out[:, 2 * m + 1] = jnp.where(low, pltpu.roll(top, L // 2, 2), bottom).astype(BF)


def kernel(
    pair_hbm, mask_ref, in_gain_ref, in_bias_ref, w_in_hbm, out_gain_ref, out_bias_ref, w_out_hbm, cot_hbm,
    dpair_hbm, gather_ref,
    pair_ref, w_in_ref, w_out_ref, cot_ref, dpair_ref, io_sem, planes,
    gains, w_in_t, w_out_t, mask_rows, in_normed, in_inv, zn,
    fa1, fa2, fb1, fb2, fgo, dmix, dxn, xn, dproj, dwout,
    out_h, in_h, out_p, in_p, plane_l, plane_r, plane_d, grad_t, work_r, work_l,
    part_out, part_in,
    w_send, w_recv, w_sum, w_all, w_full, w_gather,
    leg_s, leg_r, core_s, core_r, wt_s, wt_r,
):
    r, c = lax.axis_index("row"), lax.axis_index("col")
    q = lax.rem(r, 2)
    chip = r // 2
    y, z = chip // DEPTH, lax.rem(chip, DEPTH)
    mate = r + 1 - 2 * q
    me = chip * COLS + c
    flat = (c * 2 + y) * 2 + q

    loads = [
        pltpu.make_async_copy(src, dst, io_sem.at[n])
        for n, (src, dst) in enumerate(
            ((pair_hbm, pair_ref), (w_in_hbm, w_in_ref), (w_out_hbm, w_out_ref), (cot_hbm, cot_ref))
        )
    ]
    for load in loads:
        load.start()

    levels = [lax.rem(z + dz, DEPTH) for dz in FAR_FIRST]

    def place(k):
        return lax.rem(y + k // COLS, 2) * DEPTH, lax.rem(c + lax.rem(k, COLS), COLS)

    def near_chips(act):
        for level in levels[:-1]:
            act(y * DEPTH + level, c)

        @pl.loop(1, 16, unroll=UNROLL)
        def _(k):
            base, col = place(16 - k)
            act(base + z, col)

    def far_chips(act):
        @pl.loop(1, 16, unroll=UNROLL)
        def _(k):
            base, col = place(16 - k)
            for level in levels[:-1]:
                act(base + level, col)

    def every_chip(act):
        for level in levels[:-1]:
            act(y * DEPTH + level, c)

        @pl.loop(1, 16, unroll=UNROLL)
        def _(k):
            base, col = place(16 - k)
            for level in levels:
                act(base + level, col)

    barrier = pltpu.get_barrier_semaphore()

    def hello(semaphore, row, col):
        pl.semaphore_signal(semaphore, inc=1, device_id=(row, col), device_id_type=pl.DeviceIdType.MESH)

    near_chips(lambda to, col: hello(barrier, 2 * to + q, col))
    hello(barrier, mate, c)

    def remote(src, dst, ssem, rsem, row, col):
        return pltpu.make_async_remote_copy(
            src_ref=src, dst_ref=dst, send_sem=ssem, recv_sem=rsem,
            device_id=(row, col), device_id_type=pl.DeviceIdType.MESH,
        )

    sent = []

    def leg_send(n, src, dst, which=None):
        def send(to, col):
            remote(src.at[to * COLS + col], dst.at[me], leg_s.at[n], leg_r.at[n], 2 * to + q, col).start()

        (which or every_chip)(send)
        if which is near_chips:
            return
        pltpu.make_async_copy(src.at[me], dst.at[me], leg_r.at[n]).start()
        rest = src.at[0 : CHIPS * COLS - 1]
        sent.append(pltpu.make_async_copy(rest, rest, leg_s.at[n]).wait)

    def leg_wait(n, dst):
        pltpu.make_async_copy(dst, dst, leg_r.at[n]).wait()

    def blocks(ref):
        return ref[...].reshape(CHIPS, COLS, T, L)

    gains[0] = spread(in_gain_ref)
    gains[1] = spread(in_bias_ref)
    gains[2] = spread(out_gain_ref)
    gains[3] = spread(out_bias_ref)
    for load in loads[:3]:
        load.wait()
    w_in_t[...] = w_in_ref[...].astype(F32).T.astype(BF)
    w_out_t[...] = w_out_ref[...].astype(F32).T.astype(BF)
    mask_f = mask_ref[...].astype(F32)
    mask_rows[...] = jnp.concatenate([mask_f[0:T], mask_f[T : 2 * T]], axis=1)

    def side(t, rows, f1, f2, work):
        both = nn(w_in_t[rows : rows + 2 * L, :], zn[:, t * L : (t + 1) * L])
        value, gate = both[0:L], jax.nn.sigmoid(both[L : 2 * L])
        first = mask_rows[t : t + 1, :] * gate
        used = first * value
        f1[t] = first
        f2[t] = used * (1.0 - gate)
        work[:, t, :] = used

    for t in range(T):
        x = jnp.concatenate([pair_ref[t], pair_ref[t + T]], axis=0).T
        normed, inv = norm(x)
        in_normed[t] = normed
        in_inv[t : t + 1, :] = inv
        zn[:, t * L : (t + 1) * L] = (normed * gains[0] + gains[1]).astype(BF)
        side(t, 2 * L, fb1, fb2, work_r)
    out_h[0] = work_r[...].astype(BF)

    pl.semaphore_wait(barrier, DEPTH - 1 + 15 + 1)
    for level in levels[:-1]:
        hello(planes, 2 * (y * DEPTH + level) + q, c)
    hello(planes, mate, c)
    leg_send(0, out_h.at[0], in_p.at[0], near_chips)
    pl.semaphore_wait(planes, DEPTH)
    leg_send(0, out_h.at[0], in_p.at[0], far_chips)

    for t in range(T):
        side(t, 0, fa1, fa2, work_l)
    out_h[1] = work_l[...].astype(BF)
    leg_send(1, out_h.at[1], in_p.at[1])

    loads[3].wait()
    for t in range(T):
        gate = jax.nn.sigmoid(nn(w_in_t[4 * L : 5 * L, :], zn[:, t * L : (t + 1) * L]))
        cot = jnp.concatenate([cot_ref[t], cot_ref[t + T]], axis=0).T
        gated = cot * gate
        fgo[t] = gated * (1.0 - gate)
        mix = gated.astype(BF)
        dmix[:, t * L : (t + 1) * L] = mix
        dxn[:, t, :] = nn(w_out_ref[...], mix) * gains[2]

    leg_wait(0, in_p.at[0])
    for m in range(COLS // 2):
        plane_r[:, q, :, m * L : (m + 1) * L] = join(blocks(in_p.at[0]), m)
    swap_r = remote(plane_r.at[:, q], plane_r.at[:, q], core_s.at[0], core_r.at[0], mate, c)
    swap_r.start()
    sent.append(swap_r.wait_send)
    leg_wait(1, in_p.at[1])
    for m in range(COLS // 2):
        plane_l[:, :, m * L : (m + 1) * L] = join(blocks(in_p.at[1]), m)
    pltpu.make_async_copy(plane_r.at[:, 1 - q], plane_r.at[:, 1 - q], core_r.at[0]).wait()

    for m in range(COLS // 2):
        rows = plane_r[4 * m : 4 * m + 4].reshape(L, 512)
        split(nt(plane_l[...].reshape(256, 512), rows), out_p.at[0], m)
    leg_send(2, out_p.at[0].reshape(CHIPS * COLS, T, L), in_h.at[0])
    leg_wait(2, in_h.at[0])

    normed, inv = norm(in_h[0].astype(F32))
    work_r[...] = normed
    out_h[2] = norm_back(normed, inv, dxn[...]).astype(BF)
    leg_send(3, out_h.at[2], in_p.at[2])

    leg_wait(3, in_p.at[2])
    for m in range(COLS // 2):
        some = join(blocks(in_p.at[2]), m)
        plane_d[:, :, m * L : (m + 1) * L] = some
        grad_t[4 * m : 4 * m + 4] = some.reshape(256, L).astype(F32).T.astype(BF).reshape(4, 2, 16, 256)

    part_out[...] = nn(grad_t[:, 1 - q].reshape(256, 256), plane_l[...].reshape(256, 512)).astype(BF)
    swap_d = remote(part_out, part_in, core_s.at[1], core_r.at[1], mate, c)
    swap_d.start()
    sent.append(swap_d.wait_send)
    for m in range(COLS // 2):
        cols = plane_r[:, :, :, m * L : (m + 1) * L].reshape(512, L)
        split(nn(plane_d[...].reshape(256, 512), cols), out_p.at[1], m)
    leg_send(4, out_p.at[1].reshape(CHIPS * COLS, T, L), in_h.at[1])
    pltpu.make_async_copy(part_in, part_in, core_r.at[1]).wait()
    for m in range(COLS // 2):
        cols = plane_l[:, :, m * L : (m + 1) * L].reshape(256, L)
        own = nn(grad_t[:, q].reshape(256, 256), cols)
        split(own + part_in[:, m * L : (m + 1) * L].astype(F32), out_p.at[2], m)
    leg_send(5, out_p.at[2].reshape(CHIPS * COLS, T, L), in_h.at[2])

    for t in range(T):
        some = (work_r[:, t, :] * gains[2] + gains[3]).astype(BF)
        xn[:, t * L : (t + 1) * L] = some
        dproj[4 * L : 5 * L, t * L : (t + 1) * L] = (fgo[t] * nn(w_out_t[...], some)).astype(BF)
    dwout[...] = nt(xn[...], dmix[...])

    leg_wait(4, in_h.at[1])
    work_l[...] = in_h[1].astype(F32)
    for t in range(T):
        d = work_l[:, t, :]
        dproj[0:L, t * L : (t + 1) * L] = (d * fa1[t]).astype(BF)
        dproj[L : 2 * L, t * L : (t + 1) * L] = (d * fa2[t]).astype(BF)
    leg_wait(5, in_h.at[2])
    work_r[...] = in_h[2].astype(F32)
    for t in range(T):
        d = work_r[:, t, :]
        dproj[2 * L : 3 * L, t * L : (t + 1) * L] = (d * fb1[t]).astype(BF)
        dproj[3 * L : 4 * L, t * L : (t + 1) * L] = (d * fb2[t]).astype(BF)

    grads = jnp.concatenate([nt(zn[...], dproj[...]), dwout[...]], axis=1).astype(BF)
    w_send[:, 0] = grads[:, 0 : 3 * L].reshape(16, 8, 3 * L)
    w_send[:, 1] = grads[:, 3 * L : 6 * L].reshape(16, 8, 3 * L)

    def plane_send(copy, n):
        @pl.loop(1, 16, unroll=UNROLL)
        def _(k):
            base, col = place(16 - k)
            row, block = 2 * (base + z), col * 2 + base // DEPTH
            for core in (q, 1 - q):
                copy(block, core, row + core, col).start()

        copy(c * 2 + y, 1 - q, mate, c).start()
        sent.append(pltpu.make_async_copy(w_recv.at[0:31], w_recv.at[0:31], wt_s.at[n]).wait)

    def w1_copy(block, core, row, col):
        return remote(w_send.at[block, core], w_recv.at[flat], wt_s.at[0], wt_r.at[0], row, col)

    def w3_copy(block, core, row, col):
        return remote(w_full, w_gather.at[flat], wt_s.at[2], wt_r.at[2], row, col)

    plane_send(w1_copy, 0)
    pltpu.make_async_copy(w_send.at[c * 2 + y, q], w_recv.at[flat], wt_r.at[0]).start()

    for t in range(T):
        dn = nn(w_in_ref[...], dproj[:, t * L : (t + 1) * L]) * gains[0]
        d = norm_back(in_normed[t], in_inv[t : t + 1, :], dn).T
        dpair_ref[t] = d[0 : L // 2]
        dpair_ref[t + T] = d[L // 2 : L]

    store = pltpu.make_async_copy(dpair_ref, dpair_hbm, io_sem.at[4])
    store.start()
    pltpu.make_async_copy(w_recv, w_recv, wt_r.at[0]).wait()
    w_sum[...] = jnp.sum(w_recv[...].astype(F32), axis=0).astype(BF)
    for level in levels[:-1]:
        remote(w_sum, w_all.at[z], wt_s.at[1], wt_r.at[1], 2 * (y * DEPTH + level) + q, c).start()
    sent.append(pltpu.make_async_copy(w_all.at[1:DEPTH], w_all.at[1:DEPTH], wt_s.at[1]).wait)
    pltpu.make_async_copy(w_sum, w_all.at[z], wt_r.at[1]).start()
    pltpu.make_async_copy(w_all, w_all, wt_r.at[1]).wait()
    w_full[...] = jnp.sum(w_all[...].astype(F32), axis=0).astype(BF)
    plane_send(w3_copy, 2)
    pltpu.make_async_copy(w_full, w_gather.at[flat], wt_r.at[2]).start()
    pltpu.make_async_copy(w_gather, w_gather, wt_r.at[2]).wait()

    gather_ref[...] = w_gather[...]
    store.wait()

    for wait in sent:
        wait()


def finish_kernel(dpair_in, gather_ref, dpair_out, dwin_ref, dwout_ref):
    dpair_out[...] = dpair_in[...]

    @pl.when(pl.program_id(0) == 0)
    def _():
        whole = gather_ref[...].astype(F32).reshape(16, 2, 8, 3 * L)
        first, second = whole[:, 0].reshape(L, 3 * L), whole[:, 1].reshape(L, 3 * L)
        dwin_ref[:, 0 : 3 * L] = first
        dwin_ref[:, 3 * L : 5 * L] = second[:, 0 : 2 * L]
        dwout_ref[...] = second[:, 2 * L : 3 * L]


def body(pair, pair_mask, in_gain, in_bias, w_in, out_gain, out_bias, w_out, cotangent):
    V = pltpu.VMEM
    tile = lambda dtype: V((T, L, L), dtype)
    D = pltpu.SemaphoreType.DMA
    vmem, hbm = pl.BlockSpec(memory_space=pltpu.VMEM), pl.BlockSpec(memory_space=pl.ANY)
    d_pair, gathered = pl.pallas_call(
        kernel,
        out_shape=(jax.ShapeDtypeStruct(pair.shape, F32), jax.ShapeDtypeStruct((32, 8, 3 * L), BF)),
        in_specs=[hbm, vmem, vmem, vmem, hbm, vmem, vmem, hbm, hbm],
        out_specs=(hbm, vmem),
        scratch_shapes=[
            V(pair.shape, F32), V(w_in.shape, BF), V(w_out.shape, BF), V(pair.shape, F32), V(pair.shape, F32), D((5,)),
            pltpu.SemaphoreType.REGULAR,
            V((4, L, L), F32), V((5 * L, L), BF), V((L, L), BF), V((T, L), F32), tile(F32), V((T, L), F32), V((L, T * L), BF),
            tile(F32), tile(F32), tile(F32), tile(F32), tile(F32), V((L, T * L), BF), V((L, T, L), F32),
            V((L, T * L), BF), V((5 * L, T * L), BF), V((L, L), F32),
            V((3, L, T, L), BF), V((3, L, T, L), BF),
            V((3, CHIPS, COLS, T, L), BF), V((3, L, T, L), BF),
            V((CHIPS, 16, 512), BF), V((CHIPS, 2, 16, 512), BF), V((CHIPS, 16, 512), BF), V((CHIPS, 2, 16, 256), BF),
            V((L, T, L), F32), V((L, T, L), F32),
            V((256, 512), BF), V((256, 512), BF),
            V((16, 2, 8, 3 * L), BF), V((32, 8, 3 * L), BF), V((8, 3 * L), BF), V((DEPTH, 8, 3 * L), BF),
            V((8, 3 * L), BF), V((32, 8, 3 * L), BF),
            D((6,)), D((6,)), D((2,)), D((2,)), D((3,)), D((3,)),
        ],
        compiler_params=pltpu.CompilerParams(
            collective_id=0, has_side_effects=True, vmem_limit_bytes=60 * 1024 * 1024
        ),
    )(
        pair, pair_mask, in_gain.reshape(1, L), in_bias.reshape(1, L), w_in,
        out_gain.reshape(1, L), out_bias.reshape(1, L), w_out, cotangent,
    )
    block = pl.BlockSpec((4, 64, L), lambda n: (n, 0, 0))
    whole = lambda shape: pl.BlockSpec(shape, lambda n: (0,) * len(shape))
    return pl.pallas_call(
        finish_kernel,
        grid=(4,),
        out_shape=(
            jax.ShapeDtypeStruct(pair.shape, F32),
            jax.ShapeDtypeStruct(w_in.shape, F32),
            jax.ShapeDtypeStruct(w_out.shape, F32),
        ),
        in_specs=[block, whole((32, 8, 3 * L))],
        out_specs=(block, whole(w_in.shape), whole(w_out.shape)),
    )(d_pair, gathered)


def solution(mesh):
    placed = (
        P("row", "col", None),
        P("row", "col"),
        P(),
        P(),
        P(),
        P(),
        P(),
        P(),
        P("row", "col", None),
    )
    return jax.shard_map(
        body,
        mesh=mesh,
        in_specs=placed,
        out_specs=(P("row", "col", None), P(), P()),
        check_vma=False,
    )
```

```python
import functools

import jax
import jax.numpy as jnp
from jax import lax
from jax.experimental import pallas as pl
from jax.experimental.pallas import tpu as pltpu
from jax.sharding import PartitionSpec as P

BF = jnp.bfloat16
F32 = jnp.float32
COLS = 8
CHIPS = 16
DEPTH = 8
FAR_FIRST = (4, 3, 5, 2, 6, 1, 7, 0)
UNROLL = 3
T = 8
L = 128
EPS = 1e-05


def nn(a, b):
    return lax.dot_general(a, b, (((1,), (0,)), ((), ())), preferred_element_type=F32)


def nt(a, b):
    return lax.dot_general(a, b, (((1,), (1,)), ((), ())), preferred_element_type=F32)


def spread(vec_ref):
    return jnp.broadcast_to(vec_ref[...], (L, L)).T


def norm(x):
    cen = x - jnp.mean(x, axis=0, keepdims=True)
    inv = lax.rsqrt(jnp.mean(cen * cen, axis=0, keepdims=True) + EPS)
    return cen * inv, inv


def norm_back(normed, inv, dn):
    first = jnp.mean(dn, axis=0, keepdims=True)
    second = jnp.mean(dn * normed, axis=0, keepdims=True)
    return inv * (dn - first - normed * second)


def low_half(shape):
    return lax.broadcasted_iota(jnp.int32, shape, len(shape) - 1) < L // 2


def join(src, m):
    low = low_half((CHIPS, T, L))
    a, b = src[:, 2 * m].astype(F32), src[:, 2 * m + 1].astype(F32)
    top = jnp.where(low, a, pltpu.roll(b, L // 2, 2))
    bottom = jnp.where(low, pltpu.roll(a, L // 2, 2), b)
    return jnp.concatenate([top, bottom], axis=1).astype(BF)


def split(x, out, m):
    low = low_half((CHIPS, T, L))
    x = x.reshape(CHIPS, 2 * T, L)
    top, bottom = x[:, 0:T], x[:, T : 2 * T]
    out[:, 2 * m] = jnp.where(low, top, pltpu.roll(bottom, L // 2, 2)).astype(BF)
    out[:, 2 * m + 1] = jnp.where(low, pltpu.roll(top, L // 2, 2), bottom).astype(BF)


def kernel(
    pair_hbm, mask_ref, in_gain_ref, in_bias_ref, w_in_hbm, out_gain_ref, out_bias_ref, w_out_hbm, cot_hbm,
    dpair_hbm, gather_ref,
    pair_ref, w_in_ref, w_out_ref, cot_ref, dpair_ref, io_sem, planes,
    gains, w_in_t, w_out_t, mask_rows, in_normed, in_inv, zn,
    fa1, fa2, fb1, fb2, fgo, dmix, dxn, xn, dproj, dwout,
    out_h, in_h, out_p, in_p, plane_l, plane_r, plane_d, grad_t, work_r, work_l,
    part_out, part_in,
    send_a, recv_a, send_b, recv_b, w_sum, w_all, w_full, w_gather,
    leg_s, leg_r, core_s, core_r, wt_s, wt_r,
):
    r, c = lax.axis_index("row"), lax.axis_index("col")
    q = lax.rem(r, 2)
    chip = r // 2
    y, z = chip // DEPTH, lax.rem(chip, DEPTH)
    mate = r + 1 - 2 * q
    me = chip * COLS + c
    flat = (c * 2 + y) * 2 + q

    loads = [
        pltpu.make_async_copy(src, dst, io_sem.at[n])
        for n, (src, dst) in enumerate(
            ((pair_hbm, pair_ref), (w_in_hbm, w_in_ref), (w_out_hbm, w_out_ref), (cot_hbm, cot_ref))
        )
    ]
    for load in loads:
        load.start()

    levels = [lax.rem(z + dz, DEPTH) for dz in FAR_FIRST]

    def place(k):
        return lax.rem(y + k // COLS, 2) * DEPTH, lax.rem(c + lax.rem(k, COLS), COLS)

    def near_chips(act):
        for level in levels[:-1]:
            act(y * DEPTH + level, c)

        @pl.loop(1, 16, unroll=UNROLL)
        def _(k):
            base, col = place(16 - k)
            act(base + z, col)

    def far_chips(act):
        @pl.loop(1, 16, unroll=UNROLL)
        def _(k):
            base, col = place(16 - k)
            for level in levels[:-1]:
                act(base + level, col)

    def every_chip(act):
        for level in levels[:-1]:
            act(y * DEPTH + level, c)

        @pl.loop(1, 16, unroll=UNROLL)
        def _(k):
            base, col = place(16 - k)
            for level in levels:
                act(base + level, col)

    barrier = pltpu.get_barrier_semaphore()

    def hello(semaphore, row, col):
        pl.semaphore_signal(semaphore, inc=1, device_id=(row, col), device_id_type=pl.DeviceIdType.MESH)

    near_chips(lambda to, col: hello(barrier, 2 * to + q, col))
    hello(barrier, mate, c)

    def remote(src, dst, ssem, rsem, row, col):
        return pltpu.make_async_remote_copy(
            src_ref=src, dst_ref=dst, send_sem=ssem, recv_sem=rsem,
            device_id=(row, col), device_id_type=pl.DeviceIdType.MESH,
        )

    sent = []

    def leg_send(n, src, dst, which=None):
        def send(to, col):
            remote(src.at[to * COLS + col], dst.at[me], leg_s.at[n], leg_r.at[n], 2 * to + q, col).start()

        (which or every_chip)(send)
        if which is near_chips:
            return
        pltpu.make_async_copy(src.at[me], dst.at[me], leg_r.at[n]).start()
        rest = src.at[0 : CHIPS * COLS - 1]
        sent.append(pltpu.make_async_copy(rest, rest, leg_s.at[n]).wait)

    def leg_wait(n, dst):
        pltpu.make_async_copy(dst, dst, leg_r.at[n]).wait()

    def blocks(ref):
        return ref[...].reshape(CHIPS, COLS, T, L)

    gains[0] = spread(in_gain_ref)
    gains[1] = spread(in_bias_ref)
    gains[2] = spread(out_gain_ref)
    gains[3] = spread(out_bias_ref)
    for load in loads[:3]:
        load.wait()
    w_in_t[...] = w_in_ref[...].astype(F32).T.astype(BF)
    w_out_t[...] = w_out_ref[...].astype(F32).T.astype(BF)
    mask_f = mask_ref[...].astype(F32)
    mask_rows[...] = jnp.concatenate([mask_f[0:T], mask_f[T : 2 * T]], axis=1)

    def side(t, rows, f1, f2, work):
        both = nn(w_in_t[rows : rows + 2 * L, :], zn[:, t * L : (t + 1) * L])
        value, gate = both[0:L], jax.nn.sigmoid(both[L : 2 * L])
        first = mask_rows[t : t + 1, :] * gate
        used = first * value
        f1[t] = first
        f2[t] = used * (1.0 - gate)
        work[:, t, :] = used

    for t in range(T):
        x = jnp.concatenate([pair_ref[t], pair_ref[t + T]], axis=0).T
        normed, inv = norm(x)
        in_normed[t] = normed
        in_inv[t : t + 1, :] = inv
        zn[:, t * L : (t + 1) * L] = (normed * gains[0] + gains[1]).astype(BF)
        side(t, 2 * L, fb1, fb2, work_r)
    out_h[0] = work_r[...].astype(BF)

    pl.semaphore_wait(barrier, DEPTH - 1 + 15 + 1)
    for level in levels[:-1]:
        hello(planes, 2 * (y * DEPTH + level) + q, c)
    hello(planes, mate, c)
    leg_send(0, out_h.at[0], in_p.at[0], near_chips)
    for t in range(T):
        side(t, 0, fa1, fa2, work_l)
    out_h[1] = work_l[...].astype(BF)
    leg_send(1, out_h.at[1], in_p.at[1], near_chips)
    pl.semaphore_wait(planes, DEPTH)
    leg_send(0, out_h.at[0], in_p.at[0], far_chips)

    leg_send(1, out_h.at[1], in_p.at[1], far_chips)

    loads[3].wait()
    for t in range(T):
        gate = jax.nn.sigmoid(nn(w_in_t[4 * L : 5 * L, :], zn[:, t * L : (t + 1) * L]))
        cot = jnp.concatenate([cot_ref[t], cot_ref[t + T]], axis=0).T
        gated = cot * gate
        fgo[t] = gated * (1.0 - gate)
        mix = gated.astype(BF)
        dmix[:, t * L : (t + 1) * L] = mix
        dxn[:, t, :] = nn(w_out_ref[...], mix) * gains[2]

    leg_wait(0, in_p.at[0])
    for m in range(COLS // 2):
        plane_r[:, q, :, m * L : (m + 1) * L] = join(blocks(in_p.at[0]), m)
    swap_r = remote(plane_r.at[:, q], plane_r.at[:, q], core_s.at[0], core_r.at[0], mate, c)
    swap_r.start()
    sent.append(swap_r.wait_send)
    leg_wait(1, in_p.at[1])
    for m in range(COLS // 2):
        plane_l[:, :, m * L : (m + 1) * L] = join(blocks(in_p.at[1]), m)
    pltpu.make_async_copy(plane_r.at[:, 1 - q], plane_r.at[:, 1 - q], core_r.at[0]).wait()

    for m in range(COLS // 2):
        rows = plane_r[4 * m : 4 * m + 4].reshape(L, 512)
        split(nt(plane_l[...].reshape(256, 512), rows), out_p.at[0], m)
    leg_send(2, out_p.at[0].reshape(CHIPS * COLS, T, L), in_h.at[0])
    leg_wait(2, in_h.at[0])

    normed, inv = norm(in_h[0].astype(F32))
    work_r[...] = normed
    out_h[2] = norm_back(normed, inv, dxn[...]).astype(BF)
    leg_send(3, out_h.at[2], in_p.at[2])

    leg_wait(3, in_p.at[2])
    for m in range(COLS // 2):
        some = join(blocks(in_p.at[2]), m)
        plane_d[:, :, m * L : (m + 1) * L] = some
        grad_t[4 * m : 4 * m + 4] = some.reshape(256, L).astype(F32).T.astype(BF).reshape(4, 2, 16, 256)

    part_out[...] = nn(grad_t[:, 1 - q].reshape(256, 256), plane_l[...].reshape(256, 512)).astype(BF)
    swap_d = remote(part_out, part_in, core_s.at[1], core_r.at[1], mate, c)
    swap_d.start()
    sent.append(swap_d.wait_send)
    for m in range(COLS // 2):
        cols = plane_r[:, :, :, m * L : (m + 1) * L].reshape(512, L)
        split(nn(plane_d[...].reshape(256, 512), cols), out_p.at[1], m)
    leg_send(4, out_p.at[1].reshape(CHIPS * COLS, T, L), in_h.at[1])
    pltpu.make_async_copy(part_in, part_in, core_r.at[1]).wait()
    for m in range(COLS // 2):
        cols = plane_l[:, :, m * L : (m + 1) * L].reshape(256, L)
        own = nn(grad_t[:, q].reshape(256, 256), cols)
        split(own + part_in[:, m * L : (m + 1) * L].astype(F32), out_p.at[2], m)
    leg_send(5, out_p.at[2].reshape(CHIPS * COLS, T, L), in_h.at[2])

    for t in range(T):
        some = (work_r[:, t, :] * gains[2] + gains[3]).astype(BF)
        xn[:, t * L : (t + 1) * L] = some
        dproj[4 * L : 5 * L, t * L : (t + 1) * L] = (fgo[t] * nn(w_out_t[...], some)).astype(BF)
    dwout[...] = nt(xn[...], dmix[...])

    leg_wait(4, in_h.at[1])
    work_l[...] = in_h[1].astype(F32)
    for t in range(T):
        d = work_l[:, t, :]
        dproj[0:L, t * L : (t + 1) * L] = (d * fa1[t]).astype(BF)
        dproj[L : 2 * L, t * L : (t + 1) * L] = (d * fa2[t]).astype(BF)
    def plane_send(copy, n, whole):
        @pl.loop(1, 16, unroll=UNROLL)
        def _(k):
            base, col = place(16 - k)
            row, block = 2 * (base + z), col * 2 + base // DEPTH
            for core in (q, 1 - q):
                copy(block, core, row + core, col).start()

        copy(c * 2 + y, 1 - q, mate, c).start()
        sent.append(pltpu.make_async_copy(whole.at[0:31], whole.at[0:31], wt_s.at[n]).wait)

    def scatter(n, grads, w_send, w_recv):
        width = grads.shape[1] // 2
        w_send[:, 0] = grads[:, 0:width].astype(BF).reshape(16, 8, width)
        w_send[:, 1] = grads[:, width:].astype(BF).reshape(16, 8, width)

        def copy(block, core, row, col):
            return remote(w_send.at[block, core], w_recv.at[flat], wt_s.at[n], wt_r.at[n], row, col)

        plane_send(copy, n, w_recv)
        pltpu.make_async_copy(w_send.at[c * 2 + y, q], w_recv.at[flat], wt_r.at[n]).start()

    def w3_copy(block, core, row, col):
        return remote(w_full, w_gather.at[flat], wt_s.at[2], wt_r.at[2], row, col)

    mine = nt(zn[...], dproj[0 : 2 * L, :])
    gate = nt(zn[...], dproj[4 * L : 5 * L, :])
    scatter(0, jnp.concatenate([mine, gate, dwout[...]], axis=1), send_a, recv_a)

    leg_wait(5, in_h.at[2])
    work_r[...] = in_h[2].astype(F32)
    for t in range(T):
        d = work_r[:, t, :]
        dproj[2 * L : 3 * L, t * L : (t + 1) * L] = (d * fb1[t]).astype(BF)
        dproj[3 * L : 4 * L, t * L : (t + 1) * L] = (d * fb2[t]).astype(BF)

    scatter(3, nt(zn[...], dproj[2 * L : 4 * L, :]), send_b, recv_b)

    for t in range(T):
        dn = nn(w_in_ref[...], dproj[:, t * L : (t + 1) * L]) * gains[0]
        d = norm_back(in_normed[t], in_inv[t : t + 1, :], dn).T
        dpair_ref[t] = d[0 : L // 2]
        dpair_ref[t + T] = d[L // 2 : L]

    store = pltpu.make_async_copy(dpair_ref, dpair_hbm, io_sem.at[4])
    store.start()
    pltpu.make_async_copy(recv_a, recv_a, wt_r.at[0]).wait()
    pltpu.make_async_copy(recv_b, recv_b, wt_r.at[3]).wait()
    w_sum[:, 0 : 2 * L] = jnp.sum(recv_a[...].astype(F32), axis=0).astype(BF)
    w_sum[:, 2 * L :] = jnp.sum(recv_b[...].astype(F32), axis=0).astype(BF)
    for level in levels[:-1]:
        remote(w_sum, w_all.at[z], wt_s.at[1], wt_r.at[1], 2 * (y * DEPTH + level) + q, c).start()
    sent.append(pltpu.make_async_copy(w_all.at[1:DEPTH], w_all.at[1:DEPTH], wt_s.at[1]).wait)
    pltpu.make_async_copy(w_sum, w_all.at[z], wt_r.at[1]).start()
    pltpu.make_async_copy(w_all, w_all, wt_r.at[1]).wait()
    w_full[...] = jnp.sum(w_all[...].astype(F32), axis=0).astype(BF)
    plane_send(w3_copy, 2, w_gather)
    pltpu.make_async_copy(w_full, w_gather.at[flat], wt_r.at[2]).start()
    pltpu.make_async_copy(w_gather, w_gather, wt_r.at[2]).wait()

    gather_ref[...] = w_gather[...]
    store.wait()

    for wait in sent:
        wait()


def finish_kernel(dpair_in, gather_ref, dpair_out, dwin_ref, dwout_ref):
    dpair_out[...] = dpair_in[...]

    @pl.when(pl.program_id(0) == 0)
    def _():
        whole = gather_ref[...].astype(F32).reshape(16, 2, 8, 3 * L)
        first, second = whole[:, 0].reshape(L, 3 * L), whole[:, 1].reshape(L, 3 * L)
        dwin_ref[:, 0 : 3 * L] = first
        dwin_ref[:, 3 * L : 4 * L] = second[:, 2 * L : 3 * L]
        dwin_ref[:, 4 * L : 5 * L] = second[:, 0:L]
        dwout_ref[...] = second[:, L : 2 * L]


def body(pair, pair_mask, in_gain, in_bias, w_in, out_gain, out_bias, w_out, cotangent):
    V = pltpu.VMEM
    tile = lambda dtype: V((T, L, L), dtype)
    D = pltpu.SemaphoreType.DMA
    vmem, hbm = pl.BlockSpec(memory_space=pltpu.VMEM), pl.BlockSpec(memory_space=pl.ANY)
    d_pair, gathered = pl.pallas_call(
        kernel,
        out_shape=(jax.ShapeDtypeStruct(pair.shape, F32), jax.ShapeDtypeStruct((32, 8, 3 * L), BF)),
        in_specs=[hbm, vmem, vmem, vmem, hbm, vmem, vmem, hbm, hbm],
        out_specs=(hbm, vmem),
        scratch_shapes=[
            V(pair.shape, F32), V(w_in.shape, BF), V(w_out.shape, BF), V(pair.shape, F32), V(pair.shape, F32), D((5,)),
            pltpu.SemaphoreType.REGULAR,
            V((4, L, L), F32), V((5 * L, L), BF), V((L, L), BF), V((T, L), F32), tile(F32), V((T, L), F32), V((L, T * L), BF),
            tile(F32), tile(F32), tile(F32), tile(F32), tile(F32), V((L, T * L), BF), V((L, T, L), F32),
            V((L, T * L), BF), V((5 * L, T * L), BF), V((L, L), F32),
            V((3, L, T, L), BF), V((3, L, T, L), BF),
            V((3, CHIPS, COLS, T, L), BF), V((3, L, T, L), BF),
            V((CHIPS, 16, 512), BF), V((CHIPS, 2, 16, 512), BF), V((CHIPS, 16, 512), BF), V((CHIPS, 2, 16, 256), BF),
            V((L, T, L), F32), V((L, T, L), F32),
            V((256, 512), BF), V((256, 512), BF),
            V((16, 2, 8, 2 * L), BF), V((32, 8, 2 * L), BF), V((16, 2, 8, L), BF), V((32, 8, L), BF), V((8, 3 * L), BF), V((DEPTH, 8, 3 * L), BF),
            V((8, 3 * L), BF), V((32, 8, 3 * L), BF),
            D((6,)), D((6,)), D((2,)), D((2,)), D((4,)), D((4,)),
        ],
        compiler_params=pltpu.CompilerParams(
            collective_id=0, has_side_effects=True, vmem_limit_bytes=60 * 1024 * 1024
        ),
    )(
        pair, pair_mask, in_gain.reshape(1, L), in_bias.reshape(1, L), w_in,
        out_gain.reshape(1, L), out_bias.reshape(1, L), w_out, cotangent,
    )
    block = pl.BlockSpec((8, 64, L), lambda n: (n, 0, 0))
    whole = lambda shape: pl.BlockSpec(shape, lambda n: (0,) * len(shape))
    return pl.pallas_call(
        finish_kernel,
        grid=(2,),
        out_shape=(
            jax.ShapeDtypeStruct(pair.shape, F32),
            jax.ShapeDtypeStruct(w_in.shape, F32),
            jax.ShapeDtypeStruct(w_out.shape, F32),
        ),
        in_specs=[block, whole((32, 8, 3 * L))],
        out_specs=(block, whole(w_in.shape), whole(w_out.shape)),
    )(d_pair, gathered)


def solution(mesh):
    placed = (
        P("row", "col", None),
        P("row", "col"),
        P(),
        P(),
        P(),
        P(),
        P(),
        P(),
        P("row", "col", None),
    )
    return jax.shard_map(
        body,
        mesh=mesh,
        in_specs=placed,
        out_specs=(P("row", "col", None), P(), P()),
        check_vma=False,
    )
```

```python
import functools

import jax
import jax.numpy as jnp
from jax import lax
from jax.experimental import pallas as pl
from jax.experimental.pallas import tpu as pltpu
from jax.sharding import PartitionSpec as P

BF = jnp.bfloat16
F32 = jnp.float32
COLS = 8
CHIPS = 16
DEPTH = 8
FAR_FIRST = (4, 3, 5, 2, 6, 1, 7, 0)
UNROLL = 3
T = 8
L = 128
EPS = 1e-05


def nn(a, b):
    return lax.dot_general(a, b, (((1,), (0,)), ((), ())), preferred_element_type=F32)


def nt(a, b):
    return lax.dot_general(a, b, (((1,), (1,)), ((), ())), preferred_element_type=F32)


def spread(vec_ref):
    return jnp.broadcast_to(vec_ref[...], (L, L)).T


def norm(x):
    cen = x - jnp.mean(x, axis=0, keepdims=True)
    inv = lax.rsqrt(jnp.mean(cen * cen, axis=0, keepdims=True) + EPS)
    return cen * inv, inv


def norm_back(normed, inv, dn):
    first = jnp.mean(dn, axis=0, keepdims=True)
    second = jnp.mean(dn * normed, axis=0, keepdims=True)
    return inv * (dn - first - normed * second)


def low_half(shape):
    return lax.broadcasted_iota(jnp.int32, shape, len(shape) - 1) < L // 2


def join(src, m):
    low = low_half((CHIPS, T, L))
    a, b = src[:, 2 * m].astype(F32), src[:, 2 * m + 1].astype(F32)
    top = jnp.where(low, a, pltpu.roll(b, L // 2, 2))
    bottom = jnp.where(low, pltpu.roll(a, L // 2, 2), b)
    return jnp.concatenate([top, bottom], axis=1).astype(BF)


def split(x, out, m):
    low = low_half((CHIPS, T, L))
    x = x.reshape(CHIPS, 2 * T, L)
    top, bottom = x[:, 0:T], x[:, T : 2 * T]
    out[:, 2 * m] = jnp.where(low, top, pltpu.roll(bottom, L // 2, 2)).astype(BF)
    out[:, 2 * m + 1] = jnp.where(low, pltpu.roll(top, L // 2, 2), bottom).astype(BF)


def kernel(
    pair_hbm, mask_hbm, in_gain_hbm, in_bias_hbm, w_in_hbm, out_gain_hbm, out_bias_hbm, w_out_hbm, cot_hbm,
    dpair_hbm, gather_ref,
    pair_ref, mask_ref, in_gain_ref, in_bias_ref, w_in_ref, out_gain_ref, out_bias_ref, w_out_ref, cot_ref,
    dpair_ref, io_sem, planes,
    gains, w_in_t, w_out_t, mask_rows, in_normed, in_inv, zn,
    fa1, fa2, fb1, fb2, fgo, dmix, dxn, xn, dproj, dwout,
    out_h, in_h, out_p, in_p, plane_l, plane_r, plane_d, grad_t, work_r, work_l,
    part_out, part_in,
    send_a, recv_a, send_b, recv_b, w_sum, w_all, w_full, w_gather,
    leg_s, leg_r, core_s, core_r, wt_s, wt_r,
):
    r, c = lax.axis_index("row"), lax.axis_index("col")
    q = lax.rem(r, 2)
    chip = r // 2
    y, z = chip // DEPTH, lax.rem(chip, DEPTH)
    mate = r + 1 - 2 * q
    me = chip * COLS + c
    flat = (c * 2 + y) * 2 + q

    loads = [
        pltpu.make_async_copy(src, dst, io_sem.at[n])
        for n, (src, dst) in enumerate(
            (
                (pair_hbm, pair_ref), (mask_hbm, mask_ref), (in_gain_hbm, in_gain_ref), (in_bias_hbm, in_bias_ref),
                (w_in_hbm, w_in_ref), (out_gain_hbm, out_gain_ref), (out_bias_hbm, out_bias_ref), (w_out_hbm, w_out_ref),
                (cot_hbm, cot_ref),
            )
        )
    ]
    for load in loads:
        load.start()

    levels = [lax.rem(z + dz, DEPTH) for dz in FAR_FIRST]

    def place(k):
        return lax.rem(y + k // COLS, 2) * DEPTH, lax.rem(c + lax.rem(k, COLS), COLS)

    def near_chips(act):
        for level in levels[:-1]:
            act(y * DEPTH + level, c)

        @pl.loop(1, 16, unroll=UNROLL)
        def _(k):
            base, col = place(16 - k)
            act(base + z, col)

    def far_chips(act):
        @pl.loop(1, 16, unroll=UNROLL)
        def _(k):
            base, col = place(16 - k)
            for level in levels[:-1]:
                act(base + level, col)

    def every_chip(act):
        for level in levels[:-1]:
            act(y * DEPTH + level, c)

        @pl.loop(1, 16, unroll=UNROLL)
        def _(k):
            base, col = place(16 - k)
            for level in levels:
                act(base + level, col)

    barrier = pltpu.get_barrier_semaphore()

    def hello(semaphore, row, col):
        pl.semaphore_signal(semaphore, inc=1, device_id=(row, col), device_id_type=pl.DeviceIdType.MESH)

    near_chips(lambda to, col: hello(barrier, 2 * to + q, col))
    hello(barrier, mate, c)

    def remote(src, dst, ssem, rsem, row, col):
        return pltpu.make_async_remote_copy(
            src_ref=src, dst_ref=dst, send_sem=ssem, recv_sem=rsem,
            device_id=(row, col), device_id_type=pl.DeviceIdType.MESH,
        )

    sent = []

    def leg_send(n, src, dst, which=None):
        def send(to, col):
            remote(src.at[to * COLS + col], dst.at[me], leg_s.at[n], leg_r.at[n], 2 * to + q, col).start()

        (which or every_chip)(send)
        if which is near_chips:
            return
        pltpu.make_async_copy(src.at[me], dst.at[me], leg_r.at[n]).start()
        rest = src.at[0 : CHIPS * COLS - 1]
        sent.append(pltpu.make_async_copy(rest, rest, leg_s.at[n]).wait)

    def leg_wait(n, dst):
        pltpu.make_async_copy(dst, dst, leg_r.at[n]).wait()

    def blocks(ref):
        return ref[...].reshape(CHIPS, COLS, T, L)

    for load in loads[:8]:
        load.wait()
    gains[0] = spread(in_gain_ref)
    gains[1] = spread(in_bias_ref)
    gains[2] = spread(out_gain_ref)
    gains[3] = spread(out_bias_ref)
    w_in_t[...] = w_in_ref[...].astype(F32).T.astype(BF)
    w_out_t[...] = w_out_ref[...].astype(F32).T.astype(BF)
    mask_f = mask_ref[...].astype(F32)
    mask_rows[...] = jnp.concatenate([mask_f[0:T], mask_f[T : 2 * T]], axis=1)

    def side(t, rows, f1, f2, work):
        both = nn(w_in_t[rows : rows + 2 * L, :], zn[:, t * L : (t + 1) * L])
        value, gate = both[0:L], jax.nn.sigmoid(both[L : 2 * L])
        first = mask_rows[t : t + 1, :] * gate
        used = first * value
        f1[t] = first
        f2[t] = used * (1.0 - gate)
        work[:, t, :] = used

    for t in range(T):
        x = jnp.concatenate([pair_ref[t], pair_ref[t + T]], axis=0).T
        normed, inv = norm(x)
        in_normed[t] = normed
        in_inv[t : t + 1, :] = inv
        zn[:, t * L : (t + 1) * L] = (normed * gains[0] + gains[1]).astype(BF)
        side(t, 2 * L, fb1, fb2, work_r)
    out_h[0] = work_r[...].astype(BF)

    pl.semaphore_wait(barrier, DEPTH - 1 + 15 + 1)
    for level in levels[:-1]:
        hello(planes, 2 * (y * DEPTH + level) + q, c)
    hello(planes, mate, c)
    leg_send(0, out_h.at[0], in_p.at[0], near_chips)
    for t in range(T):
        side(t, 0, fa1, fa2, work_l)
    out_h[1] = work_l[...].astype(BF)
    leg_send(1, out_h.at[1], in_p.at[1], near_chips)
    pl.semaphore_wait(planes, DEPTH)
    leg_send(0, out_h.at[0], in_p.at[0], far_chips)

    leg_send(1, out_h.at[1], in_p.at[1], far_chips)

    loads[8].wait()
    for t in range(T):
        gate = jax.nn.sigmoid(nn(w_in_t[4 * L : 5 * L, :], zn[:, t * L : (t + 1) * L]))
        cot = jnp.concatenate([cot_ref[t], cot_ref[t + T]], axis=0).T
        gated = cot * gate
        fgo[t] = gated * (1.0 - gate)
        mix = gated.astype(BF)
        dmix[:, t * L : (t + 1) * L] = mix
        dxn[:, t, :] = nn(w_out_ref[...], mix) * gains[2]

    leg_wait(0, in_p.at[0])
    for m in range(COLS // 2):
        plane_r[:, q, :, m * L : (m + 1) * L] = join(blocks(in_p.at[0]), m)
    swap_r = remote(plane_r.at[:, q], plane_r.at[:, q], core_s.at[0], core_r.at[0], mate, c)
    swap_r.start()
    sent.append(swap_r.wait_send)
    leg_wait(1, in_p.at[1])
    for m in range(COLS // 2):
        plane_l[:, :, m * L : (m + 1) * L] = join(blocks(in_p.at[1]), m)
    pltpu.make_async_copy(plane_r.at[:, 1 - q], plane_r.at[:, 1 - q], core_r.at[0]).wait()

    for m in range(COLS // 2):
        rows = plane_r[4 * m : 4 * m + 4].reshape(L, 512)
        split(nt(plane_l[...].reshape(256, 512), rows), out_p.at[0], m)
    leg_send(2, out_p.at[0].reshape(CHIPS * COLS, T, L), in_h.at[0])
    leg_wait(2, in_h.at[0])

    normed, inv = norm(in_h[0].astype(F32))
    work_r[...] = normed
    out_h[2] = norm_back(normed, inv, dxn[...]).astype(BF)
    leg_send(3, out_h.at[2], in_p.at[2])

    leg_wait(3, in_p.at[2])
    for m in range(COLS // 2):
        some = join(blocks(in_p.at[2]), m)
        plane_d[:, :, m * L : (m + 1) * L] = some
        grad_t[4 * m : 4 * m + 4] = some.reshape(256, L).astype(F32).T.astype(BF).reshape(4, 2, 16, 256)

    part_out[...] = nn(grad_t[:, 1 - q].reshape(256, 256), plane_l[...].reshape(256, 512)).astype(BF)
    swap_d = remote(part_out, part_in, core_s.at[1], core_r.at[1], mate, c)
    swap_d.start()
    sent.append(swap_d.wait_send)
    for m in range(COLS // 2):
        cols = plane_r[:, :, :, m * L : (m + 1) * L].reshape(512, L)
        split(nn(plane_d[...].reshape(256, 512), cols), out_p.at[1], m)
    leg_send(4, out_p.at[1].reshape(CHIPS * COLS, T, L), in_h.at[1])
    pltpu.make_async_copy(part_in, part_in, core_r.at[1]).wait()
    for m in range(COLS // 2):
        cols = plane_l[:, :, m * L : (m + 1) * L].reshape(256, L)
        own = nn(grad_t[:, q].reshape(256, 256), cols)
        split(own + part_in[:, m * L : (m + 1) * L].astype(F32), out_p.at[2], m)
    leg_send(5, out_p.at[2].reshape(CHIPS * COLS, T, L), in_h.at[2])

    for t in range(T):
        some = (work_r[:, t, :] * gains[2] + gains[3]).astype(BF)
        xn[:, t * L : (t + 1) * L] = some
        dproj[4 * L : 5 * L, t * L : (t + 1) * L] = (fgo[t] * nn(w_out_t[...], some)).astype(BF)
    dwout[...] = nt(xn[...], dmix[...])

    leg_wait(4, in_h.at[1])
    work_l[...] = in_h[1].astype(F32)
    for t in range(T):
        d = work_l[:, t, :]
        dproj[0:L, t * L : (t + 1) * L] = (d * fa1[t]).astype(BF)
        dproj[L : 2 * L, t * L : (t + 1) * L] = (d * fa2[t]).astype(BF)
    def plane_send(copy, n, whole):
        @pl.loop(1, 16, unroll=UNROLL)
        def _(k):
            base, col = place(16 - k)
            row, block = 2 * (base + z), col * 2 + base // DEPTH
            for core in (q, 1 - q):
                copy(block, core, row + core, col).start()

        copy(c * 2 + y, 1 - q, mate, c).start()
        sent.append(pltpu.make_async_copy(whole.at[0:31], whole.at[0:31], wt_s.at[n]).wait)

    def scatter(n, grads, w_send, w_recv):
        width = grads.shape[1] // 2
        w_send[:, 0] = grads[:, 0:width].astype(BF).reshape(16, 8, width)
        w_send[:, 1] = grads[:, width:].astype(BF).reshape(16, 8, width)

        def copy(block, core, row, col):
            return remote(w_send.at[block, core], w_recv.at[flat], wt_s.at[n], wt_r.at[n], row, col)

        plane_send(copy, n, w_recv)
        pltpu.make_async_copy(w_send.at[c * 2 + y, q], w_recv.at[flat], wt_r.at[n]).start()

    def w3_copy(block, core, row, col):
        return remote(w_full, w_gather.at[flat], wt_s.at[2], wt_r.at[2], row, col)

    mine = nt(zn[...], dproj[0 : 2 * L, :])
    gate = nt(zn[...], dproj[4 * L : 5 * L, :])
    scatter(0, jnp.concatenate([mine, gate, dwout[...]], axis=1), send_a, recv_a)

    leg_wait(5, in_h.at[2])
    work_r[...] = in_h[2].astype(F32)
    for t in range(T):
        d = work_r[:, t, :]
        dproj[2 * L : 3 * L, t * L : (t + 1) * L] = (d * fb1[t]).astype(BF)
        dproj[3 * L : 4 * L, t * L : (t + 1) * L] = (d * fb2[t]).astype(BF)

    scatter(3, nt(zn[...], dproj[2 * L : 4 * L, :]), send_b, recv_b)

    for t in range(T):
        dn = nn(w_in_ref[...], dproj[:, t * L : (t + 1) * L]) * gains[0]
        d = norm_back(in_normed[t], in_inv[t : t + 1, :], dn).T
        dpair_ref[t] = d[0 : L // 2]
        dpair_ref[t + T] = d[L // 2 : L]

    store = pltpu.make_async_copy(dpair_ref, dpair_hbm, io_sem.at[9])
    store.start()
    pltpu.make_async_copy(recv_a, recv_a, wt_r.at[0]).wait()
    pltpu.make_async_copy(recv_b, recv_b, wt_r.at[3]).wait()
    w_sum[:, 0 : 2 * L] = jnp.sum(recv_a[...].astype(F32), axis=0).astype(BF)
    w_sum[:, 2 * L :] = jnp.sum(recv_b[...].astype(F32), axis=0).astype(BF)
    for level in levels[:-1]:
        remote(w_sum, w_all.at[z], wt_s.at[1], wt_r.at[1], 2 * (y * DEPTH + level) + q, c).start()
    sent.append(pltpu.make_async_copy(w_all.at[1:DEPTH], w_all.at[1:DEPTH], wt_s.at[1]).wait)
    pltpu.make_async_copy(w_sum, w_all.at[z], wt_r.at[1]).start()
    pltpu.make_async_copy(w_all, w_all, wt_r.at[1]).wait()
    w_full[...] = jnp.sum(w_all[...].astype(F32), axis=0).astype(BF)
    plane_send(w3_copy, 2, w_gather)
    pltpu.make_async_copy(w_full, w_gather.at[flat], wt_r.at[2]).start()
    pltpu.make_async_copy(w_gather, w_gather, wt_r.at[2]).wait()

    gather_ref[...] = w_gather[...]
    store.wait()

    for wait in sent:
        wait()


def finish_kernel(dpair_in, gather_ref, dpair_out, dwin_ref, dwout_ref):
    dpair_out[...] = dpair_in[...]

    @pl.when(pl.program_id(0) == 0)
    def _():
        whole = gather_ref[...].astype(F32).reshape(16, 2, 8, 3 * L)
        first, second = whole[:, 0].reshape(L, 3 * L), whole[:, 1].reshape(L, 3 * L)
        dwin_ref[:, 0 : 3 * L] = first
        dwin_ref[:, 3 * L : 4 * L] = second[:, 2 * L : 3 * L]
        dwin_ref[:, 4 * L : 5 * L] = second[:, 0:L]
        dwout_ref[...] = second[:, L : 2 * L]


def body(pair, pair_mask, in_gain, in_bias, w_in, out_gain, out_bias, w_out, cotangent):
    V = pltpu.VMEM
    tile = lambda dtype: V((T, L, L), dtype)
    D = pltpu.SemaphoreType.DMA
    vmem, hbm = pl.BlockSpec(memory_space=pltpu.VMEM), pl.BlockSpec(memory_space=pl.ANY)
    d_pair, gathered = pl.pallas_call(
        kernel,
        out_shape=(jax.ShapeDtypeStruct(pair.shape, F32), jax.ShapeDtypeStruct((32, 8, 3 * L), BF)),
        in_specs=[hbm] * 9,
        out_specs=(hbm, vmem),
        scratch_shapes=[
            V(pair.shape, F32), V(pair_mask.shape, jnp.int32), V((1, L), F32), V((1, L), F32), V(w_in.shape, BF),
            V((1, L), F32), V((1, L), F32), V(w_out.shape, BF), V(pair.shape, F32), V(pair.shape, F32), D((10,)),
            pltpu.SemaphoreType.REGULAR,
            V((4, L, L), F32), V((5 * L, L), BF), V((L, L), BF), V((T, L), F32), tile(F32), V((T, L), F32), V((L, T * L), BF),
            tile(F32), tile(F32), tile(F32), tile(F32), tile(F32), V((L, T * L), BF), V((L, T, L), F32),
            V((L, T * L), BF), V((5 * L, T * L), BF), V((L, L), F32),
            V((3, L, T, L), BF), V((3, L, T, L), BF),
            V((3, CHIPS, COLS, T, L), BF), V((3, L, T, L), BF),
            V((CHIPS, 16, 512), BF), V((CHIPS, 2, 16, 512), BF), V((CHIPS, 16, 512), BF), V((CHIPS, 2, 16, 256), BF),
            V((L, T, L), F32), V((L, T, L), F32),
            V((256, 512), BF), V((256, 512), BF),
            V((16, 2, 8, 2 * L), BF), V((32, 8, 2 * L), BF), V((16, 2, 8, L), BF), V((32, 8, L), BF), V((8, 3 * L), BF), V((DEPTH, 8, 3 * L), BF),
            V((8, 3 * L), BF), V((32, 8, 3 * L), BF),
            D((6,)), D((6,)), D((2,)), D((2,)), D((4,)), D((4,)),
        ],
        compiler_params=pltpu.CompilerParams(
            collective_id=0, has_side_effects=True, vmem_limit_bytes=60 * 1024 * 1024
        ),
    )(
        pair, pair_mask, in_gain.reshape(1, L), in_bias.reshape(1, L), w_in,
        out_gain.reshape(1, L), out_bias.reshape(1, L), w_out, cotangent,
    )
    block = pl.BlockSpec((8, 64, L), lambda n: (n, 0, 0))
    whole = lambda shape: pl.BlockSpec(shape, lambda n: (0,) * len(shape))
    return pl.pallas_call(
        finish_kernel,
        grid=(2,),
        out_shape=(
            jax.ShapeDtypeStruct(pair.shape, F32),
            jax.ShapeDtypeStruct(w_in.shape, F32),
            jax.ShapeDtypeStruct(w_out.shape, F32),
        ),
        in_specs=[block, whole((32, 8, 3 * L))],
        out_specs=(block, whole(w_in.shape), whole(w_out.shape)),
    )(d_pair, gathered)


def solution(mesh):
    placed = (
        P("row", "col", None),
        P("row", "col"),
        P(),
        P(),
        P(),
        P(),
        P(),
        P(),
        P("row", "col", None),
    )
    return jax.shard_map(
        body,
        mesh=mesh,
        in_specs=placed,
        out_specs=(P("row", "col", None), P(), P()),
        check_vma=False,
    )
```
